256 devices in a mesh: lon: 32 (over x_lo, z, core), lat: 4 (over y), fsdp: 2 (over x_hi).
Axes of the slice: x: 4 (x_hi: 2, x_lo: 2; x = x_hi * 2 + x_lo), y: 4, z: 8, core: 2. Of those that a mesh axis runs over, the one named last changes fastest.
Arguments:
- tokens: bfloat16 [4, 48, 384, 512], P(None, ('lat', 'fsdp'), 'lon'), may hold values from -6 to 6
- cotangent: bfloat16 [4, 48, 384, 512], P(None, ('lat', 'fsdp'), 'lon'), may hold values from -6 to 6
- qkv_weight: bfloat16 [512, 1536], P('fsdp'), may hold values from -0.25 to 0.25
- proj_weight: bfloat16 [512, 512], P('fsdp'), may hold values from -0.25 to 0.25
- norm_gain: bfloat16 [512], P('fsdp'), may hold values from 0.099609375 to 1.8984375
- shift_offsets: int32 [3], replicated, may hold values from 1 to 11, as said below
- lat_region: int32 [48], replicated, may hold values from 0 to 3, never falling along the last dimension, each value on 1 to 24 neighbouring positions
Outputs:
- block_out: bfloat16 [4, 48, 384, 512], P(None, ('lat', 'fsdp'), 'lon')
- grad_tokens: bfloat16 [4, 48, 384, 512], P(None, ('lat', 'fsdp'), 'lon')
- grad_qkv: float32 [512, 1536], P('fsdp')
- grad_proj: float32 [512, 512], P('fsdp')
- grad_gain: float32 [512], P('fsdp')
The draws below stay inside these ranges and needn't reach their ends.
Inputs may be any that keep to these rules, and one draw needn't show every extreme that they name: `shift_offsets`: entry 0 is 1; entry 1 lies in 1 to 5; entry 2 is 11. `lat_region`: labels never fall along latitude; the first row has label 0 and the last label 3.
All inputs are finite; a program needn't handle non-finite values.
Results may differ from the reference program's by a relative error of at most 0.015.
Values may be sent and summed in bfloat16 or wider, within the bound.
No kernel may reach another device: no remote copies, remote signals or barrier semaphores. Data moves between devices by JAX's collectives and lax.ppermute only.
A program may use at most 64 MiB of HBM per device.

```python
import math
import jax
import jax.numpy as jnp
import numpy as np
from jax import lax

D = 512
HEADS = 16
LEV = 4
WIN_LEV = 2
WIN_LAT = 6
WIN_LON = 12
NLAT = 48
NLON = 384


def draw_shift_offsets(key, part):
    key = jax.random.fold_in(key, 7)
    picked = jax.random.randint(key, (1,), 1, WIN_LAT, dtype=jnp.int32)
    lon_shift = jnp.full((1,), WIN_LON - 1, jnp.int32)
    return jnp.concatenate([jnp.ones((1,), jnp.int32), picked, lon_shift])


def level_of(stream_key, shape, cuts, least, largest):
    loudness = 1.0
    for dim, parts in cuts:
        draws = jax.random.uniform(jax.random.fold_in(jax.random.fold_in(stream_key, 6), dim), (parts,), jnp.float32, least / len(cuts), largest / len(cuts))
        loudness = loudness * jnp.repeat(jnp.exp(draws), shape[dim] // parts).reshape((-1,) + (1,) * (len(shape) - 1 - dim))
    return loudness


def profile(number_of, total, limit, skew):
    weights = [(1 << 20) // math.isqrt(standing ** skew) + 1 for standing in range(2, number_of + 1)]
    rest, holding = total - limit - (number_of - 1), [1] * (number_of - 1)
    while rest > 0:
        candidates = [i for i in range(number_of - 1) if holding[i] < limit]
        whole, budget = sum([weights[i] for i in candidates]), rest
        for i in candidates:
            extra = min(limit - holding[i], max(1, budget * weights[i] // whole), rest)
            holding[i] = holding[i] + extra
            rest = rest - extra
    return np.array([limit] + holding)


def ragged(key, amount, total, bound, lean):
    if amount == 2:
        one = jax.random.randint(key, (), max(1, total - bound), min(bound, total - 1) + 1)
        return jnp.stack([one, total - one])
    lengths = jnp.asarray(profile(amount, total, bound, lean), jnp.int32)
    twos = (amount - 1) // 2
    giver, receiver = lengths[1:1 + 2 * twos:2], lengths[2:2 + 2 * twos:2]
    slack = jnp.minimum(giver - 1, bound - receiver)
    moved = jax.random.randint(jax.random.fold_in(key, 1), (twos,), 0, 1 << 20) % (slack + 1)
    lengths = lengths.at[1:1 + 2 * twos:2].set(giver - moved).at[2:2 + 2 * twos:2].set(receiver + moved)
    return lengths[jax.random.permutation(jax.random.fold_in(key, 2), amount)]


def noise(key, dims, scale, limit, pieces=(), held_as=jnp.bfloat16):
    drawn = jax.random.normal(key, dims, jnp.float32) * scale
    if len(pieces) > 0:
        drawn = level_of(key, dims, pieces, -0.22, 0.18) * drawn
    return jnp.clip(drawn, min=-limit, max=limit).astype(held_as)


def setup_inputs(seed: int = 0) -> dict:
    key_of = jax.random.split(jax.random.key(seed), 8)
    tokens = noise(key_of[0], (LEV, NLAT, NLON, D), 1.0, 6.0, ((1, 8), (2, 32)))
    cotangent = noise(key_of[1], (LEV, NLAT, NLON, D), 1.0, 6.0, ((1, 8), (2, 32)))
    qkv_weight = noise(key_of[2], (D, 3 * D), D ** -0.5, 0.25, ((0, 2),))
    proj_weight = noise(key_of[3], (D, D), D ** -0.5, 0.25, ((0, 2),))
    norm_gain = jnp.clip(1.0 + 0.18 * jax.random.normal(key_of[4], (D,), jnp.float32), 0.099609375, 1.8984375).astype(jnp.bfloat16)
    shift_offsets = draw_shift_offsets(jax.random.fold_in(key_of[7], 71), 0)
    lat_region = jnp.searchsorted(jnp.cumsum(ragged(key_of[6], 4, NLAT, NLAT // 2, 0)), jnp.arange(NLAT), side="right").astype(jnp.int32)
    return {"tokens": tokens, "cotangent": cotangent, "qkv_weight": qkv_weight, "proj_weight": proj_weight, "norm_gain": norm_gain, "shift_offsets": shift_offsets, "lat_region": lat_region}


norm_eps = 1e-05

def roll_dim(array, offset, along, extent):
    doubled = jnp.concatenate([array, array], axis=along)
    return lax.dynamic_slice_in_dim(doubled, (offset % extent).astype(jnp.int32), extent, along)

def layer_norm(features, gain_f):
    average = lax.optimization_barrier(jnp.mean(features, -1, keepdims=True))
    centred = features - average
    variance = lax.optimization_barrier(jnp.mean(centred * centred, -1, keepdims=True))
    return centred * lax.rsqrt(variance + norm_eps) * gain_f

def windows_of(array):
    levels, rows, cols, feats = array.shape
    array = array.reshape(levels // WIN_LEV, WIN_LEV, rows // WIN_LAT, WIN_LAT, cols // WIN_LON, WIN_LON, feats)
    array = array.transpose(0, 2, 4, 1, 3, 5, 6)
    return array.reshape(-1, WIN_LEV * WIN_LAT * WIN_LON, feats)

def tokens_of(array, levels, rows, cols):
    feats = array.shape[-1]
    array = array.reshape(levels // WIN_LEV, rows // WIN_LAT, cols // WIN_LON, WIN_LEV, WIN_LAT, WIN_LON, feats)
    array = array.transpose(0, 3, 1, 4, 2, 5, 6)
    return array.reshape(levels, rows, cols, feats)

def attend(projected, same_region):
    windows, members, triple = projected.shape
    channels = triple // 3
    head_size = channels // HEADS
    queries = projected[..., :channels].reshape(windows, members, HEADS, head_size)
    key_rows = projected[..., channels:2 * channels].reshape(windows, members, HEADS, head_size)
    values = projected[..., 2 * channels:].reshape(windows, members, HEADS, head_size)
    scores = jnp.einsum('wqhd,wkhd->whqk', queries, key_rows, preferred_element_type=jnp.float32)
    scores = scores * (1.0 / head_size ** 0.5)
    scores = jnp.where(same_region[:, None], scores, -1e+30)
    soft = jax.nn.softmax(scores, axis=-1).astype(jnp.bfloat16)
    mixed = jnp.einsum('whqk,wkhd->wqhd', soft, values, preferred_element_type=jnp.float32)
    return mixed.astype(jnp.bfloat16).reshape(windows, members, channels)

def labels_for(lat_region, shift_offsets, row_start, rows, levels):
    lat_total = lat_region.shape[0]
    where_rows = (row_start + jnp.arange(rows, dtype=jnp.int32) + shift_offsets[1]) % lat_total
    lat_labels = jnp.take(lat_region, where_rows)
    wrapped = (jnp.arange(levels, dtype=jnp.int32) + shift_offsets[0] >= levels).astype(jnp.int32)
    return lat_labels[None, :] * 2 + wrapped[:, None]

def block_terms(shifted, shifted_cot, labels, qkv_full, proj_full, gain_full):
    levels, rows, cols, channels = shifted.shape
    features = shifted.astype(jnp.float32).reshape(-1, channels)
    normed, norm_back = jax.vjp(layer_norm, features, gain_full.astype(jnp.float32))
    hidden = normed.astype(jnp.bfloat16)
    projected = jnp.dot(hidden, qkv_full, preferred_element_type=jnp.float32).astype(jnp.bfloat16)
    label_grid = jnp.broadcast_to(labels[:, :, None, None], (levels, rows, cols, 1))
    label_win = windows_of(label_grid)[..., 0]
    same_region = label_win[:, :, None] == label_win[:, None, :]
    proj_win = windows_of(projected.reshape(levels, rows, cols, 3 * channels))
    attended, attend_back = jax.vjp(lambda packed: attend(packed, same_region), proj_win)
    mixed = tokens_of(attended, levels, rows, cols).reshape(-1, channels)
    branch = jnp.dot(mixed, proj_full, preferred_element_type=jnp.float32)
    cot_flat = shifted_cot.reshape(-1, channels)
    d_proj = jnp.einsum('td,te->de', mixed, cot_flat, preferred_element_type=jnp.float32)
    d_mixed = jnp.einsum('te,de->td', cot_flat, proj_full, preferred_element_type=jnp.float32).astype(jnp.bfloat16)
    d_win, = attend_back(windows_of(d_mixed.reshape(levels, rows, cols, channels)))
    d_projected = tokens_of(d_win, levels, rows, cols).reshape(-1, 3 * channels)
    d_qkv = jnp.einsum('td,te->de', hidden, d_projected, preferred_element_type=jnp.float32)
    d_hidden = jnp.einsum('te,de->td', d_projected, qkv_full, preferred_element_type=jnp.float32)
    d_features, d_gain = norm_back(d_hidden)
    return (branch.reshape(levels, rows, cols, channels), d_features.reshape(levels, rows, cols, channels), d_qkv, d_proj, d_gain)

def reference(tokens, cotangent, qkv_weight, proj_weight, norm_gain, shift_offsets, lat_region):
    levels, lat_total, lon_total, channels = tokens.shape

    def forward_roll(array):
        array = roll_dim(array, shift_offsets[0], 0, levels)
        array = roll_dim(array, shift_offsets[1], 1, lat_total)
        return roll_dim(array, shift_offsets[2], 2, lon_total)

    def backward_roll(array):
        array = roll_dim(array, -shift_offsets[0], 0, levels)
        array = roll_dim(array, -shift_offsets[1], 1, lat_total)
        return roll_dim(array, -shift_offsets[2], 2, lon_total)
    shifted = forward_roll(tokens)
    shifted_cot = forward_roll(cotangent)
    labels = labels_for(lat_region, shift_offsets, 0, lat_total, levels)
    blocks = lat_total // WIN_LAT
    in_blocks = shifted.reshape(levels, blocks, WIN_LAT, lon_total, channels).transpose(1, 0, 2, 3, 4)
    cot_blocks = shifted_cot.reshape(levels, blocks, WIN_LAT, lon_total, channels).transpose(1, 0, 2, 3, 4)
    label_blocks = labels.reshape(levels, blocks, WIN_LAT).transpose(1, 0, 2)

    def advance(totals, block_item):
        part_in, part_cot, part_label = block_item
        branch, d_features, d_qkv, d_proj, d_gain = block_terms(part_in, part_cot, part_label, qkv_weight, proj_weight, norm_gain)
        totals = (totals[0] + d_qkv, totals[1] + d_proj, totals[2] + d_gain)
        return (totals, (branch.astype(jnp.bfloat16), d_features.astype(jnp.bfloat16)))
    start_sums = (jnp.zeros((channels, 3 * channels), jnp.float32), jnp.zeros((channels, channels), jnp.float32), jnp.zeros((channels,), jnp.float32))
    sums, (branches, d_inputs) = lax.scan(advance, start_sums, (in_blocks, cot_blocks, label_blocks))
    branches = branches.transpose(1, 0, 2, 3, 4).reshape(levels, lat_total, lon_total, channels)
    d_inputs = d_inputs.transpose(1, 0, 2, 3, 4).reshape(levels, lat_total, lon_total, channels)
    block_out = (tokens.astype(jnp.float32) + backward_roll(branches).astype(jnp.float32)).astype(jnp.bfloat16)
    grad_tokens = (cotangent.astype(jnp.float32) + backward_roll(d_inputs).astype(jnp.float32)).astype(jnp.bfloat16)
    scaling = 1.0 / (levels * lat_total * lon_total) ** 0.5
    return (block_out, grad_tokens, sums[0] * scaling, sums[1] * scaling, sums[2] * scaling)
```

```python
import functools

import jax
import jax.numpy as jnp
from jax import lax
from jax.experimental import pallas as pl
from jax.experimental.pallas import tpu as pltpu
from jax.sharding import Mesh
from jax.sharding import PartitionSpec as P

HEADS = 16
HEAD = 32
GROUP = 8
SPAN = GROUP * HEAD
WIN_LAT = 6
WIN_LON = 12
LEVELS = 4
SLAB = WIN_LAT * WIN_LON
MEMBERS = 2 * SLAB
TOKENS = LEVELS * SLAB
PIECE_ROWS = 272
norm_eps = 1e-05

F32 = jnp.float32
BF16 = jnp.bfloat16
NN = (((1,), (0,)), ((), ()))
NT = (((1,), (1,)), ((), ()))
TN = (((0,), (0,)), ((), ()))
VM = pl.BlockSpec(memory_space=pltpu.VMEM)
SM = pl.BlockSpec(memory_space=pltpu.SMEM)


def mul(a, b, how=NN):
    return lax.dot_general(a, b, how, preferred_element_type=F32)


def sent_rows(shift):
    if shift <= WIN_LAT // 2:
        return list(range(shift)), -1
    return list(range(shift, WIN_LAT)), 1


def pack_kernel(shift, where, tok, cot, wqkv, wproj, gain, lat, lon, corner, wout):
    out_rows, _ = sent_rows(shift)
    kept = [r for r in range(WIN_LAT) if r not in out_rows]
    n, last = len(out_rows), WIN_LON - 1
    for a, src in enumerate((tok, cot)):
        for i, r in enumerate(out_rows):
            lat[pl.ds((a * n + i) * last, last)] = src[r, :last]
            corner[a * n + i] = src[r, last]
        for i, r in enumerate(kept):
            lon[a * len(kept) + i] = src[r, last]
    share = gain.shape[1]
    row = gain[...].astype(F32)
    filled = jnp.concatenate([row, jnp.zeros((1, lat.shape[2] - share), F32)], axis=1)
    lat[2 * n * last] = jnp.broadcast_to(filled, (LEVELS, lat.shape[2])).astype(BF16)
    half = wout.shape[0]
    first = pl.multiple_of(where[0] * half, half)
    wout[:, : wqkv.shape[1]] = wqkv[pl.ds(first, half), :]
    wout[:, wqkv.shape[1] :] = wproj[pl.ds(first, half), :]


def spread(block, lanes):
    zero = jnp.zeros_like(block)
    return jnp.concatenate([jnp.where(lanes == h, block, zero) for h in range(GROUP)], axis=0)


def fold(big, lanes):
    total = big[:MEMBERS]
    for h in range(1, GROUP):
        total = jnp.where(lanes == h, big[h * MEMBERS : (h + 1) * MEMBERS], total)
    return total


def label_of(member, rows, slot_is_last):
    second = (member >= SLAB).astype(jnp.int32)
    in_slab = member - SLAB * second
    label = jnp.zeros_like(member) + 2 * rows[0]
    for r in range(1, WIN_LAT):
        label = jnp.where(in_slab >= r * WIN_LON, 2 * rows[r], label)
    return label + second if slot_is_last else label


def main_kernel(
    shift, where, region, tok, cot, lat, lon, corner, wqkv, wproj, gain, wfar, wfar2,
    block, grad, rlat, rlon, rcorner, keep, send,
    xs, cs, xw, cw, wq, wp, hid, proj, dmix, mixed, dpro, ys,
):
    out_rows, side = sent_rows(shift)
    kept = [r for r in range(WIN_LAT) if r not in out_rows]
    n, last = len(out_rows), WIN_LON - 1
    channels = cw.shape[1]
    share = channels // 2
    half = share // 2
    core, f, here = where[0], where[1], where[2]

    own = pl.ds(pl.multiple_of(f * share, share), share)
    wq[own, :] = wqkv[...]
    wp[own, :] = wproj[...]
    for c, piece in ((core, wfar), (1 - core, wfar2)):
        at = pl.ds(pl.multiple_of((1 - f) * share + c * half, half), half)
        wq[at, :] = piece[:, : 3 * channels]
        wp[at, :] = piece[:, 3 * channels :]
    near = gain[...].astype(F32)
    far = lat[2 * n * last].astype(F32)[:1, :share]
    gains = jnp.concatenate(
        [jnp.where(f == 0, near, far), jnp.where(f == 0, far, near)], axis=1
    )

    for a, (src, dst) in enumerate(((tok, xs), (cot, cs))):
        for r in range(WIN_LAT):
            for c in range(WIN_LON):
                if r in out_rows:
                    i = a * n + out_rows.index(r)
                    got = lat[i * last + c] if c < last else corner[i]
                else:
                    i = a * len(kept) + kept.index(r)
                    got = src[r, c] if c < last else lon[i]
                at, got = (r * WIN_LON + c) * LEVELS, got.astype(F32)
                for q in range(channels // 128):
                    dst[q, at : at + LEVELS, :] = got[:, q * 128 : (q + 1) * 128]
    for slot in range(LEVELS):
        level = (slot + 1) % LEVELS
        at = slice(slot * SLAB, (slot + 1) * SLAB)
        for q in range(channels // 128):
            tile = slice(q * 128, (q + 1) * 128)
            xw[at, tile] = xs[q, pl.ds(level, SLAB, LEVELS), :]
            cw[at, tile] = cs[q, pl.ds(level, SLAB, LEVELS), :].astype(BF16)

    x = xw[...]
    mean = jnp.mean(x, -1, keepdims=True)
    cen = x - mean
    rstd = lax.rsqrt(jnp.mean(cen * cen, -1, keepdims=True) + norm_eps)
    hid[...] = (cen * rstd * gains).astype(BF16)
    proj[...] = mul(hid[...], wq[...]).astype(BF16)
    dmix[...] = mul(cw[...], wp[...], NT).astype(BF16)

    total = region.shape[0]
    regions = []
    for r in range(WIN_LAT):
        j = here - side if r in out_rows else here
        regions.append(region[lax.rem(j * WIN_LAT + r + total, total)])
    lane = lax.broadcasted_iota(jnp.int32, (1, GROUP * MEMBERS), 1)
    member = lane
    for h in range(1, GROUP):
        member = jnp.where(lane >= h * MEMBERS, lane - h * MEMBERS, member)
    down = lax.broadcasted_iota(jnp.int32, (MEMBERS, 1), 0)

    lanes = lax.broadcasted_iota(jnp.int32, (MEMBERS, SPAN), 1) // HEAD
    scale = 1.0 / HEAD**0.5
    to_exp2 = scale * 1.4426950408889634
    for w in range(2):
        rows = slice(w * MEMBERS, (w + 1) * MEMBERS)
        same = label_of(down, regions, w == 1) == label_of(member, regions, w == 1)
        for g in range(channels // SPAN):
            cols = slice(g * SPAN, (g + 1) * SPAN)
            kcols = slice(channels + g * SPAN, channels + (g + 1) * SPAN)
            vcols = slice(2 * channels + g * SPAN, 2 * channels + (g + 1) * SPAN)
            k, v = proj[rows, kcols], proj[rows, vcols]
            bq = spread(proj[rows, cols], lanes)
            s = jnp.where(same, mul(k, bq, NT), -1e30)
            e = jnp.exp2((s - jnp.max(s, 0, keepdims=True)) * to_exp2)
            p = e * (1.0 / jnp.sum(e, 0, keepdims=True))
            pb = p.astype(BF16)
            mixed[rows, cols] = fold(mul(pb, v, TN), lanes).astype(BF16)
            bm = spread(dmix[rows, cols], lanes)
            dp = mul(v, bm, NT)
            dpro[rows, vcols] = mul(pb, bm).astype(BF16)
            t = p * dp
            ds = ((t - p * jnp.sum(t, 0, keepdims=True)) * scale).astype(BF16)
            dpro[rows, kcols] = mul(ds, bq).astype(BF16)
            dpro[rows, cols] = fold(mul(ds, k, TN), lanes).astype(BF16)

    def give_back(values, a, base, out):
        for slot in range(LEVELS):
            for q in range(channels // 128):
                tile = values[slot * SLAB : (slot + 1) * SLAB, q * 128 : (q + 1) * 128]
                ys[q, pl.ds((slot + 1) % LEVELS, SLAB, LEVELS), :] = tile
        for r in range(WIN_LAT):
            for c in range(WIN_LON):
                at = (r * WIN_LON + c) * LEVELS
                made = jnp.concatenate(
                    [ys[q, at : at + LEVELS, :] for q in range(channels // 128)], axis=1
                )
                if r in out_rows:
                    i = a * n + out_rows.index(r)
                    if c < last:
                        rlat[i * last + c] = made.astype(BF16)
                    else:
                        rcorner[i] = made.astype(BF16)
                elif c == last:
                    rlon[a * len(kept) + kept.index(r)] = made.astype(BF16)
                else:
                    rounded = made.astype(BF16).astype(F32)
                    out[r, c] = (base[r, c].astype(F32) + rounded).astype(BF16)

    give_back(mul(mixed[...], wp[...]), 0, tok, block)

    wide, narrow = 3 * channels // 2, channels // 2
    dh = mul(dpro[...], wq[...], NT)
    xhat = (xw[...] - mean) * rstd
    dgain = jnp.sum(dh * xhat, 0, keepdims=True)
    for out, c in ((send, 1 - core), (keep, core)):
        dq = mul(hid[...], dpro[:, pl.ds(pl.multiple_of(c * wide, 128), wide)], TN)
        dw = mul(mixed[...], cw[:, pl.ds(pl.multiple_of(c * narrow, 128), narrow)], TN)
        for k in range(8):
            part = dq[:, k * 128 : (k + 1) * 128] if k < 6 else dw[:, (k - 6) * 128 : (k - 5) * 128]
            for t in range(2):
                out[k * 2 + t, :share, :] = part[t * share : (t + 1) * share].astype(BF16)
                foot = jnp.zeros((PIECE_ROWS - share, 128), F32)
                if k == 0:
                    down16 = lax.broadcasted_iota(jnp.int32, foot.shape, 0)
                    for i in range(share // 128):
                        first = t * share + i * 128
                        foot = jnp.where(down16 == i, dgain[:, first : first + 128], foot)
                out[k * 2 + t, share:, :] = foot.astype(BF16)

    dxhat = dh * gains
    low = jnp.mean(dxhat, -1, keepdims=True)
    tilt = jnp.mean(dxhat * xhat, -1, keepdims=True)
    give_back((dxhat - low - xhat * tilt) * rstd, 1, cot, grad)


def patch_kernel(shift, tok, cot, block, grad, lat, lon, corner, out_block, out_grad):
    out_rows, _ = sent_rows(shift)
    kept = [r for r in range(WIN_LAT) if r not in out_rows]
    n, last = len(out_rows), WIN_LON - 1
    for a, (base, part, out) in enumerate(((tok, block, out_block), (cot, grad, out_grad))):
        for r in range(WIN_LAT):
            if r in out_rows:
                i = a * n + out_rows.index(r)
                got = lat[pl.ds(i * last, last)].astype(F32)
                out[r, :last] = (base[r, :last].astype(F32) + got).astype(BF16)
                tail = corner[i]
            else:
                out[r, :last] = part[r, :last]
                tail = lon[a * len(kept) + kept.index(r)]
            out[r, last] = (base[r, last].astype(F32) + tail.astype(F32)).astype(BF16)


def finish_kernel(scaling, where, near, far, gqkv, gproj, ggain):
    core = where[0]
    share, wide = gqkv.shape[0], gqkv.shape[1] // 2
    narrow = gproj.shape[1] // 2
    for part, c in ((near, core), (far, 1 - core)):
        for k in range(8):
            made = part[k, :share, :].astype(F32) * scaling
            if k < 6:
                gqkv[:, pl.ds(pl.multiple_of(c * wide + k * 128, 128), 128)] = made
            else:
                gproj[:, pl.ds(pl.multiple_of(c * narrow + (k - 6) * 128, 128), 128)] = made
    foot = near[0, share:, :].astype(F32) * scaling
    ggain[...] = jnp.concatenate([foot[i : i + 1] for i in range(share // 128)], axis=1)


def call(kernel, outs, ins, scratch=(), limit=16 << 20):
    return pl.pallas_call(
        kernel,
        out_shape=outs,
        in_specs=ins,
        out_specs=[VM] * len(outs),
        scratch_shapes=list(scratch),
        compiler_params=pltpu.CompilerParams(vmem_limit_bytes=limit),
    )


def ring(count, by):
    return [(i, (i + by) % count) for i in range(count)]


def across(sizes, axes, move):
    pairs = []
    count = 1
    for a in axes:
        count *= sizes[a]
    for flat in range(count):
        rest, at = flat, {}
        for a in reversed(axes):
            at[a], rest = rest % sizes[a], rest // sizes[a]
        goal = move(dict(at))
        to = 0
        for a in axes:
            to = to * sizes[a] + goal[a]
        pairs.append((flat, to))
    return pairs


def step(shift, sizes, tokens, cotangent, wqkv, wproj, gain, region):
    out_rows, side = sent_rows(shift)
    n, kept, last = len(out_rows), WIN_LAT - len(out_rows), WIN_LON - 1
    channels = tokens.shape[-1]
    share = channels // 2
    lon, lat = ("xl", "z", "c"), ("y", "xh")
    lon_count = sizes["xl"] * sizes["z"] * sizes["c"]
    lat_count = sizes["y"] * sizes["xh"]
    both = lon + lat

    def diagonal(by_lon, by_lat):
        return [
            (o * lat_count + j, ((o + by_lon) % lon_count) * lat_count + (j + by_lat) % lat_count)
            for o in range(lon_count)
            for j in range(lat_count)
        ]

    struct = jax.ShapeDtypeStruct
    where = jnp.stack([lax.axis_index("c"), lax.axis_index("xh"), lax.axis_index(lat)]).astype(jnp.int32)
    gain2 = gain.reshape(1, share)
    shapes = [
        struct((2 * n * last + 1, LEVELS, channels), BF16),
        struct((2 * kept, LEVELS, channels), BF16),
        struct((2 * n, LEVELS, channels), BF16),
    ]
    mlat, mlon, mcorner, wout = call(
        functools.partial(pack_kernel, shift),
        shapes + [struct((share // 2, 4 * channels), BF16)],
        [SM] + [VM] * 5,
    )(where, tokens, cotangent, wqkv, wproj, gain2)

    swap = [(0, 1), (1, 0)]
    other_chip = across(sizes, ("xl", "xh"), lambda at: {"xl": 1 - at["xl"], "xh": 1 - at["xh"]})
    wfar = lax.ppermute(wout, ("xl", "xh"), other_chip)
    mlat = lax.ppermute(mlat, lat, ring(lat_count, side))
    mlon = lax.ppermute(mlon, lon, ring(lon_count, 1))
    mcorner = lax.ppermute(mcorner, both, diagonal(1, side))
    wfar2 = lax.ppermute(wfar, "c", swap)

    grid = struct(tokens.shape, BF16)
    pieces = struct((16, PIECE_ROWS, 128), BF16)
    block, grad, rlat, rlon, rcorner, keep, send = call(
        functools.partial(main_kernel, shift),
        [grid, grid, struct((2 * n * last, LEVELS, channels), BF16)] + shapes[1:] + [pieces, pieces],
        [SM, SM] + [VM] * 10,
        [
            pltpu.VMEM((channels // 128, TOKENS, 128), F32),
            pltpu.VMEM((channels // 128, TOKENS, 128), F32),
            pltpu.VMEM((TOKENS, channels), F32),
            pltpu.VMEM((TOKENS, channels), BF16),
            pltpu.VMEM((channels, 3 * channels), BF16),
            pltpu.VMEM((channels, channels), BF16),
            pltpu.VMEM((TOKENS, channels), BF16),
            pltpu.VMEM((TOKENS, 3 * channels), BF16),
            pltpu.VMEM((TOKENS, channels), BF16),
            pltpu.VMEM((TOKENS, channels), BF16),
            pltpu.VMEM((TOKENS, 3 * channels), BF16),
            pltpu.VMEM((channels // 128, TOKENS, 128), F32),
        ],
        40 << 20,
    )(where, region, tokens, cotangent, mlat, mlon, mcorner, wqkv, wproj, gain2, wfar, wfar2)

    arrived = lax.ppermute(send, "c", swap)
    rlat = lax.ppermute(rlat, lat, ring(lat_count, -side))
    rlon = lax.ppermute(rlon, lon, ring(lon_count, -1))
    rcorner = lax.ppermute(rcorner, both, diagonal(-1, -side))
    pair = (keep.astype(F32) + arrived.astype(F32)).astype(BF16)
    plane = lax.all_to_all(pair, ("y", "xl", "xh"), 0, 0, tiled=True)
    piece = jnp.sum(plane.astype(F32), 0).astype(BF16)
    column = jnp.broadcast_to(piece, (sizes["z"],) + piece.shape)
    column = lax.all_to_all(column, "z", 0, 0, tiled=True)
    piece = jnp.sum(column.astype(F32), 0).astype(BF16)
    near = lax.all_to_all(jnp.broadcast_to(piece, (8,) + piece.shape), ("y", "xl"), 0, 0, tiled=True)
    far = lax.ppermute(near, "c", swap)

    out_block, out_grad = call(
        functools.partial(patch_kernel, shift), [grid, grid], [VM] * 7
    )(tokens, cotangent, block, grad, rlat, rlon, rcorner)
    scaling = 1.0 / (TOKENS * lon_count * lat_count) ** 0.5
    gqkv, gproj, ggain = call(
        functools.partial(finish_kernel, scaling),
        [struct((share, 3 * channels), F32), struct((share, channels), F32), struct((1, share), F32)],
        [SM, VM, VM],
    )(where, near, far)
    return out_block, out_grad, gqkv, gproj, ggain.reshape(share)


def on_device(sizes, tokens, cotangent, wqkv, wproj, gain, shift_offsets, region):
    tokens = tokens.transpose(1, 2, 0, 3)
    cotangent = cotangent.transpose(1, 2, 0, 3)
    out = lax.switch(
        shift_offsets[1] - 1,
        [functools.partial(step, shift, sizes) for shift in range(1, WIN_LAT)],
        tokens, cotangent, wqkv, wproj, gain, region,
    )
    return out[0].transpose(2, 0, 1, 3), out[1].transpose(2, 0, 1, 3), out[2], out[3], out[4]


def solution(mesh):
    lon, lat, fsdp = (mesh.shape[a] for a in ("lon", "lat", "fsdp"))
    sizes = {"xl": 2, "z": lon // 4, "c": 2, "y": lat, "xh": fsdp}
    fine = Mesh(mesh.devices.reshape(tuple(sizes.values())), tuple(sizes))
    grid = P(None, ("y", "xh"), ("xl", "z", "c"), None)
    rows = P("xh", None)
    return jax.shard_map(
        functools.partial(on_device, sizes),
        mesh=fine,
        in_specs=(grid, grid, rows, rows, P("xh"), P(), P()),
        out_specs=(grid, grid, rows, rows, P("xh")),
        check_vma=False,
    )
```

```python
import functools

import jax
import jax.numpy as jnp
from jax import lax
from jax.experimental import pallas as pl
from jax.experimental.pallas import tpu as pltpu
from jax.sharding import Mesh
from jax.sharding import PartitionSpec as P

HEADS = 16
HEAD = 32
GROUP = 8
SPAN = GROUP * HEAD
WIN_LAT = 6
WIN_LON = 12
LEVELS = 4
SLAB = WIN_LAT * WIN_LON
MEMBERS = 2 * SLAB
TOKENS = LEVELS * SLAB
COLUMNS = 8
norm_eps = 1e-05

F32 = jnp.float32
BF16 = jnp.bfloat16
NN = (((1,), (0,)), ((), ()))
NT = (((1,), (1,)), ((), ()))
TN = (((0,), (0,)), ((), ()))
VM = pl.BlockSpec(memory_space=pltpu.VMEM)
SM = pl.BlockSpec(memory_space=pltpu.SMEM)
HBM = pl.BlockSpec(memory_space=pltpu.HBM)


def mul(a, b, how=NN):
    return lax.dot_general(a, b, how, preferred_element_type=F32)


def pack_kernel(where, tok, cot, wqkv, wproj, gain, lat, lon, corner, wout, sems):
    last, most = WIN_LON - 1, WIN_LAT - 1
    part, wide = wout.shape[0], wqkv.shape[1]
    rows = pl.ds(pl.multiple_of(where[3] * part, part), part)
    moves = [
        (wqkv.at[rows, :], wout.at[:, pl.ds(0, wide)]),
        (wproj.at[rows, :], wout.at[:, pl.ds(wide, wout.shape[1] - wide)]),
    ]
    for a, src in enumerate((tok, cot)):
        moves.append((src.at[pl.ds(0, most), pl.ds(0, last)], lat.at[a]))
        moves.append((src.at[:, last], lon.at[a]))
        moves.append((src.at[pl.ds(0, most), last], corner.at[pl.ds(a * most, most)]))
    copies = [pltpu.make_async_copy(src, dst, sems.at[i]) for i, (src, dst) in enumerate(moves)]
    for copy in copies:
        copy.start()
    share, channels = gain.shape[0], corner.shape[2]
    row = gain[...].astype(F32).reshape(1, share)
    filled = jnp.concatenate([row, jnp.zeros((1, channels - share), F32)], axis=1)
    corner[2 * most] = jnp.broadcast_to(filled, (LEVELS, channels)).astype(BF16)
    for copy in copies:
        copy.wait()


def spread(block, lanes):
    zero = jnp.zeros_like(block)
    return jnp.concatenate([jnp.where(lanes == h, block, zero) for h in range(GROUP)], axis=0)


def fold(big, lanes):
    total = big[:MEMBERS]
    for h in range(1, GROUP):
        total = jnp.where(lanes == h, big[h * MEMBERS : (h + 1) * MEMBERS], total)
    return total


def label_of(member, rows, slot_is_last):
    second = (member >= SLAB).astype(jnp.int32)
    in_slab = member - SLAB * second
    label = jnp.zeros_like(member) + 2 * rows[0]
    for r in range(1, WIN_LAT):
        label = jnp.where(in_slab >= r * WIN_LON, 2 * rows[r], label)
    return label + second if slot_is_last else label


def main_kernel(
    where, shifts, region, tok, cot, lat, lon, corner, wqkv, wproj, gain, wfar, wfar2,
    block, grad, rlat, rlon, rcorner, keep, send,
    xs, cs, xw, cw, wq, wp, hid, proj, dmix, mixed, dpro, ys,
):
    last = WIN_LON - 1
    channels = cw.shape[1]
    share = channels // 2
    half = share // 2
    core, f, here = where[0], where[1], where[2]

    own = pl.ds(pl.multiple_of(f * share, share), share)
    wq[own, :] = wqkv[...]
    wp[own, :] = wproj[...]
    for c, piece in ((core, wfar), (1 - core, wfar2)):
        at = pl.ds(pl.multiple_of((1 - f) * share + c * half, half), half)
        wq[at, :] = piece[:, : 3 * channels]
        wp[at, :] = piece[:, 3 * channels :]
    near = gain[...].astype(F32).reshape(1, share)
    far = corner[2 * (WIN_LAT - 1)].astype(F32)[:1, :share]
    gains = jnp.concatenate(
        [jnp.where(f == 0, near, far), jnp.where(f == 0, far, near)], axis=1
    )

    def put(dst, r, c, got):
        at, got = (r * WIN_LON + c) * LEVELS, got.astype(F32)
        for q in range(channels // 128):
            dst[q, at : at + LEVELS, :] = got[:, q * 128 : (q + 1) * 128]

    most, by = WIN_LAT - 1, shifts[1]
    for r in range(WIN_LAT):
        if r < most:

            @pl.when(r < by)
            def _(r=r):
                for a, dst in enumerate((xs, cs)):
                    for c in range(last):
                        put(dst, r, c, lat[a, r, c])
                    put(dst, r, last, corner[a * most + r])

        @pl.when(r >= by)
        def _(r=r):
            for a, (src, dst) in enumerate(((tok, xs), (cot, cs))):
                for c in range(last):
                    put(dst, r, c, src[r, c])
                put(dst, r, last, lon[a, r])

    for slot in range(LEVELS):
        level = (slot + 1) % LEVELS
        at = slice(slot * SLAB, (slot + 1) * SLAB)
        for q in range(channels // 128):
            tile = slice(q * 128, (q + 1) * 128)
            xw[at, tile] = xs[q, pl.ds(level, SLAB, LEVELS), :]
            cw[at, tile] = cs[q, pl.ds(level, SLAB, LEVELS), :].astype(BF16)

    x = xw[...]
    mean = jnp.mean(x, -1, keepdims=True)
    cen = x - mean
    rstd = lax.rsqrt(jnp.mean(cen * cen, -1, keepdims=True) + norm_eps)
    hid[...] = (cen * rstd * gains).astype(BF16)
    proj[...] = mul(hid[...], wq[...]).astype(BF16)
    dmix[...] = mul(cw[...], wp[...], NT).astype(BF16)

    total = region.shape[0]
    regions = []
    for r in range(WIN_LAT):
        j = here + jnp.where(r < by, 1, 0)
        regions.append(region[lax.rem(j * WIN_LAT + r + total, total)])
    lane = lax.broadcasted_iota(jnp.int32, (1, GROUP * MEMBERS), 1)
    member = lane
    for h in range(1, GROUP):
        member = jnp.where(lane >= h * MEMBERS, lane - h * MEMBERS, member)
    down = lax.broadcasted_iota(jnp.int32, (MEMBERS, 1), 0)

    lanes = lax.broadcasted_iota(jnp.int32, (MEMBERS, SPAN), 1) // HEAD
    scale = 1.0 / HEAD**0.5
    to_exp2 = scale * 1.4426950408889634
    for w in range(2):
        rows = slice(w * MEMBERS, (w + 1) * MEMBERS)
        same = label_of(down, regions, w == 1) == label_of(member, regions, w == 1)
        for g in range(channels // SPAN):
            cols = slice(g * SPAN, (g + 1) * SPAN)
            kcols = slice(channels + g * SPAN, channels + (g + 1) * SPAN)
            vcols = slice(2 * channels + g * SPAN, 2 * channels + (g + 1) * SPAN)
            k, v = proj[rows, kcols], proj[rows, vcols]
            bq = spread(proj[rows, cols], lanes)
            s = jnp.where(same, mul(k, bq, NT), -1e30)
            e = jnp.exp2((s - jnp.max(s, 0, keepdims=True)) * to_exp2)
            p = e * (1.0 / jnp.sum(e, 0, keepdims=True))
            pb = p.astype(BF16)
            mixed[rows, cols] = fold(mul(pb, v, TN), lanes).astype(BF16)
            bm = spread(dmix[rows, cols], lanes)
            dp = mul(v, bm, NT)
            dpro[rows, vcols] = mul(pb, bm).astype(BF16)
            t = p * dp
            ds = ((t - p * jnp.sum(t, 0, keepdims=True)) * scale).astype(BF16)
            dpro[rows, kcols] = mul(ds, bq).astype(BF16)
            dpro[rows, cols] = fold(mul(ds, k, TN), lanes).astype(BF16)

    def give_back(values, a, base, out):
        for slot in range(LEVELS):
            for q in range(channels // 128):
                tile = values[slot * SLAB : (slot + 1) * SLAB, q * 128 : (q + 1) * 128]
                ys[q, pl.ds((slot + 1) % LEVELS, SLAB, LEVELS), :] = tile
        def made(r, c):
            at = (r * WIN_LON + c) * LEVELS
            tiles = [ys[q, at : at + LEVELS, :] for q in range(channels // 128)]
            return jnp.concatenate(tiles, axis=1).astype(BF16)

        for r in range(WIN_LAT):
            if r < most:

                @pl.when(r < by)
                def _(r=r):
                    for c in range(last):
                        rlat[a, r, c] = made(r, c)
                    rcorner[a * most + r] = made(r, last)

            @pl.when(r >= by)
            def _(r=r):
                for c in range(last):
                    out[r, c] = (base[r, c].astype(F32) + made(r, c).astype(F32)).astype(BF16)
                rlon[a, r] = made(r, last)

    give_back(mul(mixed[...], wp[...]), 0, tok, block)

    wide, narrow = 3 * channels // 2, channels // 2
    for out, c in ((send, 1 - core), (keep, core)):
        dq = mul(hid[...], dpro[:, pl.ds(pl.multiple_of(c * wide, 128), wide)], TN)
        dw = mul(mixed[...], cw[:, pl.ds(pl.multiple_of(c * narrow, 128), narrow)], TN)
        for k in range(COLUMNS):
            part = dq[:, k * 128 : (k + 1) * 128] if k < 6 else dw[:, (k - 6) * 128 : (k - 5) * 128]
            for t in range(2):
                for z in range(2):
                    first = t * share + z * half
                    out[(z * COLUMNS + k) * 2 + t] = part[first : first + half].astype(BF16)

    dh = mul(dpro[...], wq[...], NT)
    xhat = (xw[...] - mean) * rstd
    dxhat = dh * gains
    low = jnp.mean(dxhat, -1, keepdims=True)
    tilt = jnp.mean(dxhat * xhat, -1, keepdims=True)
    give_back((dxhat - low - xhat * tilt) * rstd, 1, cot, grad)


def patch_kernel(shifts, tok, cot, block, grad, lat, lon, corner, out_block, out_grad):
    last, most, by = WIN_LON - 1, WIN_LAT - 1, shifts[1]
    for a, (base, part, out) in enumerate(((tok, block, out_block), (cot, grad, out_grad))):
        for r in range(WIN_LAT):
            if r < most:

                @pl.when(r < by)
                def _(a=a, base=base, out=out, r=r):
                    got = lat[a, r].astype(F32)
                    out[r, :last] = (base[r, :last].astype(F32) + got).astype(BF16)
                    got = corner[a * most + r].astype(F32)
                    out[r, last] = (base[r, last].astype(F32) + got).astype(BF16)

            @pl.when(r >= by)
            def _(a=a, base=base, part=part, out=out, r=r):
                out[r, :last] = part[r, :last]
                got = lon[a, r].astype(F32)
                out[r, last] = (base[r, last].astype(F32) + got).astype(BF16)


def finish_kernel(scaling, where, near, far, wqkv, gain, gqkv, gproj, ggain):
    core = where[0]
    share, wide = gqkv.shape[0], gqkv.shape[1] // 2
    half, narrow = share // 2, gproj.shape[1] // 2
    for z in range(2):
        rows = slice(z * half, (z + 1) * half)
        total = jnp.zeros((half, 128), F32)
        for part, c in ((near, core), (far, 1 - core)):
            for k in range(COLUMNS):
                made = part[z * COLUMNS + k].astype(F32) * scaling
                if k < 6:
                    at = pl.ds(pl.multiple_of(c * wide + k * 128, 128), 128)
                    gqkv[rows, at] = made
                    total = total + made * wqkv[rows, at].astype(F32)
                else:
                    gproj[rows, pl.ds(pl.multiple_of(c * narrow + (k - 6) * 128, 128), 128)] = made
        over = jnp.sum(total.T, 0, keepdims=True)
        gains = gain[...].astype(F32).reshape(1, share)[:, rows]
        ggain[rows] = (over / gains).reshape(half)


def call(kernel, outs, ins, scratch=(), limit=16 << 20, moved=1 << 20):
    return pl.pallas_call(
        kernel,
        out_shape=outs,
        in_specs=ins,
        out_specs=[VM] * len(outs),
        scratch_shapes=list(scratch),
        compiler_params=pltpu.CompilerParams(vmem_limit_bytes=limit),
        cost_estimate=pl.CostEstimate(flops=0, bytes_accessed=moved, transcendentals=0),
    )


def ring(count, by):
    return [(i, (i + by) % count) for i in range(count)]


LON, LAT = ("xl", "zh", "zl", "c"), ("y", "xh")
SWAP = [(0, 1), (1, 0)]
BESIDE = [(0, 3), (3, 0), (1, 2), (2, 1)]


def diagonal(lon_count, by_lon, lat_count, by_lat):
    return [
        (o * lat_count + j, ((o + by_lon) % lon_count) * lat_count + (j + by_lat) % lat_count)
        for o in range(lon_count)
        for j in range(lat_count)
    ]


def on_device(sizes, tokens, cotangent, wqkv, wproj, gain, shifts, region):
    tokens = tokens.transpose(1, 2, 0, 3)
    cotangent = cotangent.transpose(1, 2, 0, 3)
    last = WIN_LON - 1
    channels = tokens.shape[-1]
    share = channels // 2
    lon_count = sizes["xl"] * sizes["zh"] * sizes["zl"] * sizes["c"]
    lat_count = sizes["y"] * sizes["xh"]

    struct = jax.ShapeDtypeStruct
    where = jnp.stack([lax.axis_index(a) for a in ("c", "xh", LAT, ("c", "zl", "y"))]).astype(jnp.int32)
    most = WIN_LAT - 1
    mlat = struct((2, most, last, LEVELS, channels), BF16)
    mlon = struct((2, WIN_LAT, LEVELS, channels), BF16)
    mcorner = struct((2 * most + 1, LEVELS, channels), BF16)
    lat, lon, corner, wout = call(
        pack_kernel,
        [mlat, mlon, mcorner, struct((share // 16, 4 * channels), BF16)],
        [SM] + [HBM] * 4 + [VM],
        [pltpu.SemaphoreType.DMA((8,))],
    )(where, tokens, cotangent, wqkv, wproj, gain)

    wnext = lax.ppermute(wout, ("xl", "xh"), BESIDE)
    wnext, lat, lon, corner = lax.optimization_barrier((wnext, lat, lon, corner))
    lat = lax.ppermute(lat, LAT, ring(lat_count, -1))
    lon = lax.ppermute(lon, LON, ring(lon_count, 1))
    corner = lax.ppermute(corner, LON + LAT, diagonal(lon_count, 1, lat_count, -1))
    wnext = jnp.broadcast_to(wnext, (8,) + wnext.shape)
    wfar = lax.all_to_all(wnext, ("zl", "y"), 0, 0, tiled=True)
    wfar, lat, lon, corner = lax.optimization_barrier((wfar, lat, lon, corner))
    wfar = wfar.reshape(-1, wfar.shape[-1])
    wfar2 = lax.ppermute(wfar, "c", SWAP)

    grid = struct(tokens.shape, BF16)
    pieces = struct((4 * COLUMNS, share // 2, 128), BF16)
    block, grad, rlat, rlon, rcorner, keep, send = call(
        main_kernel,
        [grid, grid, mlat, mlon, mcorner, pieces, pieces],
        [SM, SM, SM] + [VM] * 10,
        [
            pltpu.VMEM((channels // 128, TOKENS, 128), F32),
            pltpu.VMEM((channels // 128, TOKENS, 128), F32),
            pltpu.VMEM((TOKENS, channels), F32),
            pltpu.VMEM((TOKENS, channels), BF16),
            pltpu.VMEM((channels, 3 * channels), BF16),
            pltpu.VMEM((channels, channels), BF16),
            pltpu.VMEM((TOKENS, channels), BF16),
            pltpu.VMEM((TOKENS, 3 * channels), BF16),
            pltpu.VMEM((TOKENS, channels), BF16),
            pltpu.VMEM((TOKENS, channels), BF16),
            pltpu.VMEM((TOKENS, 3 * channels), BF16),
            pltpu.VMEM((channels // 128, TOKENS, 128), F32),
        ],
        32 << 20,
    )(where, shifts, region, tokens, cotangent, lat, lon, corner, wqkv, wproj, gain, wfar, wfar2)

    pair = (keep.astype(F32) + lax.ppermute(send, "c", SWAP).astype(F32)).astype(BF16)
    spread_out = lax.all_to_all(pair, ("zl", "y", "xl", "xh"), 0, 0, tiled=True)
    piece = jnp.sum(spread_out.astype(F32), 0).astype(BF16)
    piece, rlat, rlon, rcorner = lax.optimization_barrier((piece, rlat, rlon, rcorner))
    rlat = lax.ppermute(rlat, LAT, ring(lat_count, 1))
    others = [lax.ppermute(piece, "zh", ring(4, by)) for by in (1, 2, 3)]
    rlon = lax.ppermute(rlon, LON, ring(lon_count, -1))
    rcorner = lax.ppermute(rcorner, LON + LAT, diagonal(lon_count, -1, lat_count, 1))
    others, rlat, rlon, rcorner = lax.optimization_barrier((others, rlat, rlon, rcorner))
    piece = (piece.astype(F32) + sum(p.astype(F32) for p in others)).astype(BF16)
    near = lax.all_to_all(
        jnp.broadcast_to(piece, (2 * COLUMNS,) + piece.shape), ("zl", "y", "xl"), 0, 0, tiled=True
    )
    far = lax.ppermute(near, "c", SWAP)

    out_block, out_grad = call(patch_kernel, [grid, grid], [SM] + [VM] * 7, moved=4 << 20)(
        shifts, tokens, cotangent, block, grad, rlat, rlon, rcorner
    )
    scaling = 1.0 / (TOKENS * lon_count * lat_count) ** 0.5
    gqkv, gproj, ggain = call(
        functools.partial(finish_kernel, scaling),
        [struct((share, 3 * channels), F32), struct((share, channels), F32), struct((share,), F32)],
        [SM] + [VM] * 4,
    )(where, near, far, wqkv, gain)
    return out_block.transpose(2, 0, 1, 3), out_grad.transpose(2, 0, 1, 3), gqkv, gproj, ggain


def solution(mesh):
    lon, lat, fsdp = (mesh.shape[a] for a in ("lon", "lat", "fsdp"))
    sizes = {"xl": 2, "zh": lon // 8, "zl": 2, "c": 2, "y": lat, "xh": fsdp}
    fine = Mesh(mesh.devices.reshape(tuple(sizes.values())), tuple(sizes))
    grid = P(None, LAT, LON, None)
    rows = P("xh", None)
    return jax.shard_map(
        functools.partial(on_device, sizes),
        mesh=fine,
        in_specs=(grid, grid, rows, rows, P("xh"), P(), P()),
        out_specs=(grid, grid, rows, rows, P("xh")),
        check_vma=False,
    )
```

```python
import functools

import jax
import jax.numpy as jnp
from jax import lax
from jax.experimental import pallas as pl
from jax.experimental.pallas import tpu as pltpu
from jax.sharding import Mesh
from jax.sharding import PartitionSpec as P

HEADS = 16
HEAD = 32
GROUP = 8
SPAN = GROUP * HEAD
WIN_LAT = 6
WIN_LON = 12
LEVELS = 4
SLAB = WIN_LAT * WIN_LON
MEMBERS = 2 * SLAB
TOKENS = LEVELS * SLAB
COLUMNS = 8
norm_eps = 1e-05

F32 = jnp.float32
BF16 = jnp.bfloat16
NN = (((1,), (0,)), ((), ()))
NT = (((1,), (1,)), ((), ()))
TN = (((0,), (0,)), ((), ()))
VM = pl.BlockSpec(memory_space=pltpu.VMEM)
SM = pl.BlockSpec(memory_space=pltpu.SMEM)


def mul(a, b, how=NN):
    return lax.dot_general(a, b, how, preferred_element_type=F32)


def spread(block, lanes):
    zero = jnp.zeros_like(block)
    return jnp.concatenate([jnp.where(lanes == h, block, zero) for h in range(GROUP)], axis=0)


def fold(big, lanes):
    total = big[:MEMBERS]
    for h in range(1, GROUP):
        total = jnp.where(lanes == h, big[h * MEMBERS : (h + 1) * MEMBERS], total)
    return total


def label_of(member, rows, slot_is_last):
    second = (member >= SLAB).astype(jnp.int32)
    in_slab = member - SLAB * second
    label = jnp.zeros_like(member) + 2 * rows[0]
    for r in range(1, WIN_LAT):
        label = jnp.where(in_slab >= r * WIN_LON, 2 * rows[r], label)
    return label + second if slot_is_last else label


def main_kernel(
    where, shifts, region, tok, cot, lat0, lat1, lon, corner, wqkv, wproj, gain, wx, wy, wcx, wcy,
    block, grad, rlat, rlon, rcorner, keep, send,
    xs, cs, xw, cw, wq, wp, hid, proj, dmix, mixed, dpro, ys,
):
    last = WIN_LON - 1
    channels = cw.shape[1]
    share = channels // 2
    half = share // 2
    core, f, here = where[0], where[1], where[2]

    own = pl.ds(pl.multiple_of(f * share, share), share)
    wq[own, :] = wqkv[...]
    wp[own, :] = wproj[...]
    quarter, at_x = wx.shape[0], where[3]
    for place, piece in ((at_x, wx), (at_x ^ 1, wy), (at_x ^ 2, wcx), (at_x ^ 3, wcy)):
        at = pl.ds(pl.multiple_of((1 - f) * share + place * quarter, quarter), quarter)
        wq[at, :] = piece[:, : 3 * channels]
        wp[at, :] = piece[:, 3 * channels :]
    near = gain[...].astype(F32).reshape(1, share)
    far = corner[2 * (WIN_LAT - 1)].astype(F32)[:1, :share]
    gains = jnp.concatenate(
        [jnp.where(f == 0, near, far), jnp.where(f == 0, far, near)], axis=1
    )

    def put(dst, r, c, got):
        at, got = (r * WIN_LON + c) * LEVELS, got.astype(F32)
        for q in range(channels // 128):
            dst[q, at : at + LEVELS, :] = got[:, q * 128 : (q + 1) * 128]

    most, by = WIN_LAT - 1, shifts[1]
    for r in range(WIN_LAT):
        if r < most:

            @pl.when(r < by)
            def _(r=r):
                for a, dst in enumerate((xs, cs)):
                    for c in range(last):
                        early = lat0.shape[1]
                        put(dst, r, c, lat0[a, r, c] if r < early else lat1[a, r - early, c])
                    put(dst, r, last, corner[a * most + r])

        @pl.when(r >= by)
        def _(r=r):
            for a, (src, dst) in enumerate(((tok, xs), (cot, cs))):
                for c in range(last):
                    put(dst, r, c, src[r, c])
                put(dst, r, last, lon[a, r])

    for slot in range(LEVELS):
        level = (slot + 1) % LEVELS
        at = slice(slot * SLAB, (slot + 1) * SLAB)
        for q in range(channels // 128):
            tile = slice(q * 128, (q + 1) * 128)
            xw[at, tile] = xs[q, pl.ds(level, SLAB, LEVELS), :]
            cw[at, tile] = cs[q, pl.ds(level, SLAB, LEVELS), :].astype(BF16)

    x = xw[...]
    mean = jnp.mean(x, -1, keepdims=True)
    cen = x - mean
    rstd = lax.rsqrt(jnp.mean(cen * cen, -1, keepdims=True) + norm_eps)
    hid[...] = (cen * rstd * gains).astype(BF16)
    proj[...] = mul(hid[...], wq[...]).astype(BF16)
    dmix[...] = mul(cw[...], wp[...], NT).astype(BF16)

    total = region.shape[0]
    regions = []
    for r in range(WIN_LAT):
        j = here + jnp.where(r < by, 1, 0)
        regions.append(region[lax.rem(j * WIN_LAT + r + total, total)])
    lane = lax.broadcasted_iota(jnp.int32, (1, GROUP * MEMBERS), 1)
    member = lane
    for h in range(1, GROUP):
        member = jnp.where(lane >= h * MEMBERS, lane - h * MEMBERS, member)
    down = lax.broadcasted_iota(jnp.int32, (MEMBERS, 1), 0)

    lanes = lax.broadcasted_iota(jnp.int32, (MEMBERS, SPAN), 1) // HEAD
    scale = 1.0 / HEAD**0.5
    to_exp2 = scale * 1.4426950408889634
    for w in range(2):
        rows = slice(w * MEMBERS, (w + 1) * MEMBERS)
        same = label_of(down, regions, w == 1) == label_of(member, regions, w == 1)
        for g in range(channels // SPAN):
            cols = slice(g * SPAN, (g + 1) * SPAN)
            kcols = slice(channels + g * SPAN, channels + (g + 1) * SPAN)
            vcols = slice(2 * channels + g * SPAN, 2 * channels + (g + 1) * SPAN)
            k, v = proj[rows, kcols], proj[rows, vcols]
            bq = spread(proj[rows, cols], lanes)
            s = jnp.where(same, mul(k, bq, NT), -1e30)
            e = jnp.exp2((s - jnp.max(s, 0, keepdims=True)) * to_exp2)
            p = e * (1.0 / jnp.sum(e, 0, keepdims=True))
            pb = p.astype(BF16)
            mixed[rows, cols] = fold(mul(pb, v, TN), lanes).astype(BF16)
            bm = spread(dmix[rows, cols], lanes)
            dp = mul(v, bm, NT)
            dpro[rows, vcols] = mul(pb, bm).astype(BF16)
            t = p * dp
            ds = ((t - p * jnp.sum(t, 0, keepdims=True)) * scale).astype(BF16)
            dpro[rows, kcols] = mul(ds, bq).astype(BF16)
            dpro[rows, cols] = fold(mul(ds, k, TN), lanes).astype(BF16)

    def give_back(values, a, base, out):
        for slot in range(LEVELS):
            for q in range(channels // 128):
                tile = values[slot * SLAB : (slot + 1) * SLAB, q * 128 : (q + 1) * 128]
                ys[q, pl.ds((slot + 1) % LEVELS, SLAB, LEVELS), :] = tile
        def made(r, c):
            at = (r * WIN_LON + c) * LEVELS
            tiles = [ys[q, at : at + LEVELS, :] for q in range(channels // 128)]
            return jnp.concatenate(tiles, axis=1).astype(BF16)

        for r in range(WIN_LAT):
            if r < most:

                @pl.when(r < by)
                def _(r=r):
                    for c in range(last):
                        rlat[a, r, c] = made(r, c)
                    rcorner[a * most + r] = made(r, last)

            @pl.when(r >= by)
            def _(r=r):
                for c in range(last):
                    out[r, c] = (base[r, c].astype(F32) + made(r, c).astype(F32)).astype(BF16)
                rlon[a, r] = made(r, last)

    give_back(mul(mixed[...], wp[...]), 0, tok, block)

    wide, narrow = 3 * channels // 2, channels // 2
    for out, c in ((send, 1 - core), (keep, core)):
        dq = mul(hid[...], dpro[:, pl.ds(pl.multiple_of(c * wide, 128), wide)], TN)
        dw = mul(mixed[...], cw[:, pl.ds(pl.multiple_of(c * narrow, 128), narrow)], TN)
        for k in range(COLUMNS):
            part = dq[:, k * 128 : (k + 1) * 128] if k < 6 else dw[:, (k - 6) * 128 : (k - 5) * 128]
            for t in range(2):
                for z in range(2):
                    first = t * share + z * half
                    out[(z * COLUMNS + k) * 2 + t] = part[first : first + half].astype(BF16)

    dh = mul(dpro[...], wq[...], NT)
    xhat = (xw[...] - mean) * rstd
    dxhat = dh * gains
    low = jnp.mean(dxhat, -1, keepdims=True)
    tilt = jnp.mean(dxhat * xhat, -1, keepdims=True)
    give_back((dxhat - low - xhat * tilt) * rstd, 1, cot, grad)


def patch_kernel(shifts, tok, cot, block, grad, lat, lon, corner, out_block, out_grad):
    last, most, by = WIN_LON - 1, WIN_LAT - 1, shifts[1]
    for a, (base, part, out) in enumerate(((tok, block, out_block), (cot, grad, out_grad))):
        for r in range(WIN_LAT):
            if r < most:

                @pl.when(r < by)
                def _(a=a, base=base, out=out, r=r):
                    got = lat[a, r].astype(F32)
                    out[r, :last] = (base[r, :last].astype(F32) + got).astype(BF16)
                    got = corner[a * most + r].astype(F32)
                    out[r, last] = (base[r, last].astype(F32) + got).astype(BF16)

            @pl.when(r >= by)
            def _(a=a, base=base, part=part, out=out, r=r):
                out[r, :last] = part[r, :last]
                got = lon[a, r].astype(F32)
                out[r, last] = (base[r, last].astype(F32) + got).astype(BF16)


def finish_kernel(scaling, where, near, far, wqkv, gain, gqkv, gproj, ggain):
    core = where[0]
    rows, wide = gqkv.shape[0], gqkv.shape[1] // 2
    narrow = gproj.shape[1] // 2
    total = jnp.zeros((rows, 128), F32)
    for part, c in ((near, core), (far, 1 - core)):
        for k in range(COLUMNS):
            made = part[k].astype(F32) * scaling
            if k < 6:
                at = pl.ds(pl.multiple_of(c * wide + k * 128, 128), 128)
                gqkv[:, at] = made
                total = total + made * wqkv[:, at].astype(F32)
            else:
                gproj[:, pl.ds(pl.multiple_of(c * narrow + (k - 6) * 128, 128), 128)] = made
    over = jnp.sum(total.T, 0, keepdims=True)
    ggain[...] = over / gain[...].astype(F32)


def call(kernel, outs, ins, scratch=(), limit=16 << 20, moved=1 << 20):
    return pl.pallas_call(
        kernel,
        out_shape=outs,
        in_specs=ins,
        out_specs=[VM] * len(outs),
        scratch_shapes=list(scratch),
        compiler_params=pltpu.CompilerParams(vmem_limit_bytes=limit),
        cost_estimate=pl.CostEstimate(flops=0, bytes_accessed=moved, transcendentals=0),
    )


def ring(count, by):
    return [(i, (i + by) % count) for i in range(count)]


LON, LAT = ("xl", "zh", "zl", "c"), ("y", "xh")
SWAP = [(0, 1), (1, 0)]
BESIDE = [(0, 3), (3, 0), (1, 2), (2, 1)]


def diagonal(lon_count, by_lon, lat_count, by_lat):
    return [
        (o * lat_count + j, ((o + by_lon) % lon_count) * lat_count + (j + by_lat) % lat_count)
        for o in range(lon_count)
        for j in range(lat_count)
    ]


def main_call(where, shifts, region, tokens, cotangent, lat0, lat1, lon, corner, wqkv, wproj, gain, *others):
    struct = jax.ShapeDtypeStruct
    channels, share = tokens.shape[-1], wqkv.shape[0]
    grid = struct(tokens.shape, BF16)
    pieces = struct((4 * COLUMNS, share // 2, 128), BF16)
    rlat = struct((2, WIN_LAT - 1, WIN_LON - 1, LEVELS, channels), BF16)
    rcorner = struct((2 * (WIN_LAT - 1), LEVELS, channels), BF16)
    return call(
        main_kernel,
        [grid, grid, rlat, struct(lon.shape, BF16), rcorner, pieces, pieces],
        [SM, SM, SM] + [VM] * 13,
        [
            pltpu.VMEM((channels // 128, TOKENS, 128), F32),
            pltpu.VMEM((channels // 128, TOKENS, 128), F32),
            pltpu.VMEM((TOKENS, channels), F32),
            pltpu.VMEM((TOKENS, channels), BF16),
            pltpu.VMEM((channels, 3 * channels), BF16),
            pltpu.VMEM((channels, channels), BF16),
            pltpu.VMEM((TOKENS, channels), BF16),
            pltpu.VMEM((TOKENS, 3 * channels), BF16),
            pltpu.VMEM((TOKENS, channels), BF16),
            pltpu.VMEM((TOKENS, channels), BF16),
            pltpu.VMEM((TOKENS, 3 * channels), BF16),
            pltpu.VMEM((channels // 128, TOKENS, 128), F32),
        ],
        32 << 20,
    )(where, shifts, region, tokens, cotangent, lat0, lat1, lon, corner, wqkv, wproj, gain, *others)


def on_device(sizes, tokens, cotangent, wqkv, wproj, gain, shifts, region):
    tokens = tokens.transpose(1, 2, 0, 3)
    cotangent = cotangent.transpose(1, 2, 0, 3)
    last = WIN_LON - 1
    channels = tokens.shape[-1]
    share = channels // 2
    lon_count = sizes["xl"] * sizes["zh"] * sizes["zl"] * sizes["c"]
    lat_count = sizes["y"] * sizes["xh"]

    struct = jax.ShapeDtypeStruct
    where = jnp.stack([lax.axis_index(a) for a in ("c", "xh", LAT, "y")]).astype(jnp.int32)
    where = where.at[3].set(2 * where[0] + lax.rem(where[3], 2))
    most = WIN_LAT - 1
    part = share // 4
    wout = jnp.concatenate(
        [lax.dynamic_slice_in_dim(w, where[3] * part, part, 0) for w in (wqkv, wproj)], axis=1
    )
    early = 2
    wx = lax.ppermute(wout, ("xl", "xh"), BESIDE)
    lat = [
        jnp.stack([a[rows, :last] for a in (tokens, cotangent)])
        for rows in (slice(0, early), slice(early, most))
    ]
    lat[0] = lax.ppermute(lat[0], LAT, ring(lat_count, -1))
    lon = jnp.stack([a[:, last] for a in (tokens, cotangent)])
    foot = jnp.pad(gain.reshape(1, 1, share), ((0, 0), (0, LEVELS - 1), (0, channels - share)))
    corner = jnp.concatenate([tokens[:most, last], cotangent[:most, last], foot])
    wx, lat, lon, corner = lax.optimization_barrier((wx, lat, lon, corner))
    wy = lax.ppermute(wx, "y", [(i, i ^ 1) for i in range(sizes["y"])])
    lat[1] = lax.ppermute(lat[1], LAT, ring(lat_count, -1))
    lon = lax.ppermute(lon, LON, ring(lon_count, 1))
    corner = lax.ppermute(corner, LON + LAT, diagonal(lon_count, 1, lat_count, -1))
    wcx = lax.ppermute(wx, "c", SWAP)
    wy, wcx, lat, lon, corner = lax.optimization_barrier((wy, wcx, lat, lon, corner))
    wcy = lax.ppermute(wy, "c", SWAP)

    grid = struct(tokens.shape, BF16)
    block, grad, rlat, rlon, rcorner, keep, send = main_call(
        where, shifts, region, tokens, cotangent, *lat, lon, corner, wqkv, wproj, gain, wx, wy, wcx, wcy
    )

    pair = (keep.astype(F32) + lax.ppermute(send, "c", SWAP).astype(F32)).astype(BF16)
    plane = lax.all_to_all(pair, ("zl", "y", "xl", "xh"), 0, 0, tiled=True)
    piece = jnp.sum(plane.astype(F32), 0).astype(BF16)
    rlat = lax.ppermute(rlat, LAT, ring(lat_count, 1))
    others = [lax.ppermute(piece, "zh", ring(4, by)) for by in (1, 2, 3)]
    rlon = lax.ppermute(rlon, LON, ring(lon_count, -1))
    rcorner = lax.ppermute(rcorner, LON + LAT, diagonal(lon_count, -1, lat_count, 1))
    others, rlat, rlon, rcorner = lax.optimization_barrier((others, rlat, rlon, rcorner))
    piece = (piece.astype(F32) + sum(p.astype(F32) for p in others)).astype(BF16)
    near = lax.all_to_all(
        jnp.broadcast_to(piece, (2 * COLUMNS,) + piece.shape), ("zl", "y", "xl"), 0, 0, tiled=True
    )
    far = lax.ppermute(near, "c", SWAP)

    out_block, out_grad = call(patch_kernel, [grid, grid], [SM] + [VM] * 7, moved=4 << 20)(
        shifts, tokens, cotangent, block, grad, rlat, rlon, rcorner
    )
    scaling = 1.0 / (TOKENS * lon_count * lat_count) ** 0.5
    half = share // 2
    of_rows = lambda z: (z, 0)
    of_pieces = pl.BlockSpec((COLUMNS, half, 128), lambda z: (z, 0, 0))
    of_gain = pl.BlockSpec((1, half), lambda z: (0, z))
    gqkv, gproj, ggain = pl.pallas_call(
        functools.partial(finish_kernel, scaling),
        grid=(2,),
        out_shape=[struct((share, 3 * channels), F32), struct((share, channels), F32), struct((1, share), F32)],
        in_specs=[SM, of_pieces, of_pieces, pl.BlockSpec((half, 3 * channels), of_rows), of_gain],
        out_specs=[
            pl.BlockSpec((half, 3 * channels), of_rows),
            pl.BlockSpec((half, channels), of_rows),
            of_gain,
        ],
        compiler_params=pltpu.CompilerParams(vmem_limit_bytes=16 << 20),
    )(where, near, far, wqkv, gain.reshape(1, share))
    return out_block.transpose(2, 0, 1, 3), out_grad.transpose(2, 0, 1, 3), gqkv, gproj, ggain.reshape(share)


def solution(mesh):
    lon, lat, fsdp = (mesh.shape[a] for a in ("lon", "lat", "fsdp"))
    sizes = {"xl": 2, "zh": lon // 8, "zl": 2, "c": 2, "y": lat, "xh": fsdp}
    fine = Mesh(mesh.devices.reshape(tuple(sizes.values())), tuple(sizes))
    grid = P(None, LAT, LON, None)
    rows = P("xh", None)
    return jax.shard_map(
        functools.partial(on_device, sizes),
        mesh=fine,
        in_specs=(grid, grid, rows, rows, P("xh"), P(), P()),
        out_specs=(grid, grid, rows, rows, P("xh")),
        check_vma=False,
    )
```

```python
import functools

import jax
import jax.numpy as jnp
from jax import lax
from jax.experimental import pallas as pl
from jax.experimental.pallas import tpu as pltpu
from jax.sharding import Mesh
from jax.sharding import PartitionSpec as P

HEADS = 16
HEAD = 32
GROUP = 8
SPAN = GROUP * HEAD
WIN_LAT = 6
WIN_LON = 12
LEVELS = 4
SLAB = WIN_LAT * WIN_LON
MEMBERS = 2 * SLAB
TOKENS = LEVELS * SLAB
COLUMNS = 8
norm_eps = 1e-05

F32 = jnp.float32
BF16 = jnp.bfloat16
NN = (((1,), (0,)), ((), ()))
NT = (((1,), (1,)), ((), ()))
TN = (((0,), (0,)), ((), ()))
VM = pl.BlockSpec(memory_space=pltpu.VMEM)
SM = pl.BlockSpec(memory_space=pltpu.SMEM)


def mul(a, b, how=NN):
    return lax.dot_general(a, b, how, preferred_element_type=F32)


def spread(block, lanes):
    zero = jnp.zeros_like(block)
    return jnp.concatenate([jnp.where(lanes == h, block, zero) for h in range(GROUP)], axis=0)


def fold(big, lanes):
    total = big[:MEMBERS]
    for h in range(1, GROUP):
        total = jnp.where(lanes == h, big[h * MEMBERS : (h + 1) * MEMBERS], total)
    return total


def label_of(member, rows, slot_is_last):
    second = (member >= SLAB).astype(jnp.int32)
    in_slab = member - SLAB * second
    label = jnp.zeros_like(member) + 2 * rows[0]
    for r in range(1, WIN_LAT):
        label = jnp.where(in_slab >= r * WIN_LON, 2 * rows[r], label)
    return label + second if slot_is_last else label


def main_kernel(
    where, shifts, region, tok, cot, lat0, lat1, lon, corner, wqkv, wproj, gain, wx, wz, wcx, wcz,
    block, grad, rlat, rlon, rcorner, keep, send,
    xs, cs, xw, cw, wq, wp, hid, proj, dmix, mixed, dpro, ys,
):
    last = WIN_LON - 1
    channels = cw.shape[1]
    share = channels // 2
    half = share // 2
    core, f, here = where[0], where[1], where[2]

    own = pl.ds(pl.multiple_of(f * share, share), share)
    wq[own, :] = wqkv[...]
    wp[own, :] = wproj[...]
    quarter, at_x = wx.shape[0], where[3]
    for place, piece in ((at_x, wx), (at_x ^ 1, wz), (at_x ^ 2, wcx), (at_x ^ 3, wcz)):
        at = pl.ds(pl.multiple_of((1 - f) * share + place * quarter, quarter), quarter)
        wq[at, :] = piece[:, : 3 * channels]
        wp[at, :] = piece[:, 3 * channels :]
    near = gain[...].astype(F32).reshape(1, share)
    far = corner[2 * (WIN_LAT - 1)].astype(F32)[:1, :share]
    gains = jnp.concatenate(
        [jnp.where(f == 0, near, far), jnp.where(f == 0, far, near)], axis=1
    )

    def put(dst, r, c, got):
        at, got = (r * WIN_LON + c) * LEVELS, got.astype(F32)
        for q in range(channels // 128):
            dst[q, at : at + LEVELS, :] = got[:, q * 128 : (q + 1) * 128]

    most, by = WIN_LAT - 1, shifts[1]
    for r in range(WIN_LAT):
        if r < most:

            @pl.when(r < by)
            def _(r=r):
                for a, dst in enumerate((xs, cs)):
                    for c in range(last):
                        early = lat0.shape[1]
                        put(dst, r, c, lat0[a, r, c] if r < early else lat1[a, r - early, c])
                    put(dst, r, last, corner[a * most + r])

        @pl.when(r >= by)
        def _(r=r):
            for a, (src, dst) in enumerate(((tok, xs), (cot, cs))):
                for c in range(last):
                    put(dst, r, c, src[r, c])
                put(dst, r, last, lon[a, r])

    for slot in range(LEVELS):
        level = (slot + 1) % LEVELS
        at = slice(slot * SLAB, (slot + 1) * SLAB)
        for q in range(channels // 128):
            tile = slice(q * 128, (q + 1) * 128)
            xw[at, tile] = xs[q, pl.ds(level, SLAB, LEVELS), :]
            cw[at, tile] = cs[q, pl.ds(level, SLAB, LEVELS), :].astype(BF16)

    x = xw[...]
    mean = jnp.mean(x, -1, keepdims=True)
    cen = x - mean
    rstd = lax.rsqrt(jnp.mean(cen * cen, -1, keepdims=True) + norm_eps)
    hid[...] = (cen * rstd * gains).astype(BF16)
    proj[...] = mul(hid[...], wq[...]).astype(BF16)
    dmix[...] = mul(cw[...], wp[...], NT).astype(BF16)

    total = region.shape[0]
    regions = []
    for r in range(WIN_LAT):
        j = here + jnp.where(r < by, 1, 0)
        regions.append(region[lax.rem(j * WIN_LAT + r + total, total)])
    lane = lax.broadcasted_iota(jnp.int32, (1, GROUP * MEMBERS), 1)
    member = lane
    for h in range(1, GROUP):
        member = jnp.where(lane >= h * MEMBERS, lane - h * MEMBERS, member)
    down = lax.broadcasted_iota(jnp.int32, (MEMBERS, 1), 0)

    lanes = lax.broadcasted_iota(jnp.int32, (MEMBERS, SPAN), 1) // HEAD
    scale = 1.0 / HEAD**0.5
    to_exp2 = scale * 1.4426950408889634
    for w in range(2):
        rows = slice(w * MEMBERS, (w + 1) * MEMBERS)
        same = label_of(down, regions, w == 1) == label_of(member, regions, w == 1)
        for g in range(channels // SPAN):
            cols = slice(g * SPAN, (g + 1) * SPAN)
            kcols = slice(channels + g * SPAN, channels + (g + 1) * SPAN)
            vcols = slice(2 * channels + g * SPAN, 2 * channels + (g + 1) * SPAN)
            k, v = proj[rows, kcols], proj[rows, vcols]
            bq = spread(proj[rows, cols], lanes)
            s = jnp.where(same, mul(k, bq, NT), -1e30)
            e = jnp.exp2((s - jnp.max(s, 0, keepdims=True)) * to_exp2)
            p = e * (1.0 / jnp.sum(e, 0, keepdims=True))
            pb = p.astype(BF16)
            mixed[rows, cols] = fold(mul(pb, v, TN), lanes).astype(BF16)
            bm = spread(dmix[rows, cols], lanes)
            dp = mul(v, bm, NT)
            dpro[rows, vcols] = mul(pb, bm).astype(BF16)
            t = p * dp
            ds = ((t - p * jnp.sum(t, 0, keepdims=True)) * scale).astype(BF16)
            dpro[rows, kcols] = mul(ds, bq).astype(BF16)
            dpro[rows, cols] = fold(mul(ds, k, TN), lanes).astype(BF16)

    def give_back(values, a, base, out):
        for slot in range(LEVELS):
            for q in range(channels // 128):
                tile = values[slot * SLAB : (slot + 1) * SLAB, q * 128 : (q + 1) * 128]
                ys[q, pl.ds((slot + 1) % LEVELS, SLAB, LEVELS), :] = tile
        def made(r, c):
            at = (r * WIN_LON + c) * LEVELS
            tiles = [ys[q, at : at + LEVELS, :] for q in range(channels // 128)]
            return jnp.concatenate(tiles, axis=1).astype(BF16)

        for r in range(WIN_LAT):
            if r < most:

                @pl.when(r < by)
                def _(r=r):
                    for c in range(last):
                        rlat[a, r, c] = made(r, c)
                    rcorner[a * most + r] = made(r, last)

            @pl.when(r >= by)
            def _(r=r):
                for c in range(last):
                    out[r, c] = (base[r, c].astype(F32) + made(r, c).astype(F32)).astype(BF16)
                rlon[a, r] = made(r, last)

    give_back(mul(mixed[...], wp[...]), 0, tok, block)

    wide, narrow = 3 * channels // 2, channels // 2
    for out, c in ((send, 1 - core), (keep, core)):
        dq = mul(hid[...], dpro[:, pl.ds(pl.multiple_of(c * wide, 128), wide)], TN)
        dw = mul(mixed[...], cw[:, pl.ds(pl.multiple_of(c * narrow, 128), narrow)], TN)
        for k in range(COLUMNS):
            part = dq[:, k * 128 : (k + 1) * 128] if k < 6 else dw[:, (k - 6) * 128 : (k - 5) * 128]
            for t in range(2):
                for z in range(2):
                    first = t * share + z * half
                    out[(z * COLUMNS + k) * 2 + t] = part[first : first + half].astype(BF16)

    dh = mul(dpro[...], wq[...], NT)
    xhat = (xw[...] - mean) * rstd
    dxhat = dh * gains
    low = jnp.mean(dxhat, -1, keepdims=True)
    tilt = jnp.mean(dxhat * xhat, -1, keepdims=True)
    give_back((dxhat - low - xhat * tilt) * rstd, 1, cot, grad)


def patch_kernel(shifts, tok, cot, block, grad, lat, lon, corner, out_block, out_grad):
    last, most, by = WIN_LON - 1, WIN_LAT - 1, shifts[1]
    for a, (base, part, out) in enumerate(((tok, block, out_block), (cot, grad, out_grad))):
        for r in range(WIN_LAT):
            if r < most:

                @pl.when(r < by)
                def _(a=a, base=base, out=out, r=r):
                    got = lat[a, r].astype(F32)
                    out[r, :last] = (base[r, :last].astype(F32) + got).astype(BF16)
                    got = corner[a * most + r].astype(F32)
                    out[r, last] = (base[r, last].astype(F32) + got).astype(BF16)

            @pl.when(r >= by)
            def _(a=a, base=base, part=part, out=out, r=r):
                out[r, :last] = part[r, :last]
                got = lon[a, r].astype(F32)
                out[r, last] = (base[r, last].astype(F32) + got).astype(BF16)


def finish_kernel(scaling, where, near, far, wqkv, gain, gqkv, gproj, ggain):
    core = where[0]
    rows, wide = gqkv.shape[0], gqkv.shape[1] // 2
    narrow = gproj.shape[1] // 2
    total = jnp.zeros((rows, 128), F32)
    for part, c in ((near, core), (far, 1 - core)):
        for k in range(COLUMNS):
            made = part[k].astype(F32) * scaling
            if k < 6:
                at = pl.ds(pl.multiple_of(c * wide + k * 128, 128), 128)
                gqkv[:, at] = made
                total = total + made * wqkv[:, at].astype(F32)
            else:
                gproj[:, pl.ds(pl.multiple_of(c * narrow + (k - 6) * 128, 128), 128)] = made
    over = jnp.sum(total.T, 0, keepdims=True)
    ggain[...] = over / gain[...].astype(F32)


def call(kernel, outs, ins, scratch=(), limit=12 << 20, moved=1 << 20):
    return pl.pallas_call(
        kernel,
        out_shape=outs,
        in_specs=ins,
        out_specs=[VM] * len(outs),
        scratch_shapes=list(scratch),
        compiler_params=pltpu.CompilerParams(vmem_limit_bytes=limit),
        cost_estimate=pl.CostEstimate(flops=0, bytes_accessed=moved, transcendentals=0),
    )


def ring(count, by):
    return [(i, (i + by) % count) for i in range(count)]


LON, LAT = ("xl", "zh", "zl", "c"), ("y", "xh")
SWAP = [(0, 1), (1, 0)]
BESIDE = [(0, 3), (3, 0), (1, 2), (2, 1)]


def diagonal(lon_count, by_lon, lat_count, by_lat):
    return [
        (o * lat_count + j, ((o + by_lon) % lon_count) * lat_count + (j + by_lat) % lat_count)
        for o in range(lon_count)
        for j in range(lat_count)
    ]


def main_call(where, shifts, region, tokens, cotangent, lat0, lat1, lon, corner, wqkv, wproj, gain, *others):
    struct = jax.ShapeDtypeStruct
    channels, share = tokens.shape[-1], wqkv.shape[0]
    grid = struct(tokens.shape, BF16)
    pieces = struct((4 * COLUMNS, share // 2, 128), BF16)
    rlat = struct((2, WIN_LAT - 1, WIN_LON - 1, LEVELS, channels), BF16)
    rcorner = struct((2 * (WIN_LAT - 1), LEVELS, channels), BF16)
    return call(
        main_kernel,
        [grid, grid, rlat, struct(lon.shape, BF16), rcorner, pieces, pieces],
        [SM, SM, SM] + [VM] * 13,
        [
            pltpu.VMEM((channels // 128, TOKENS, 128), F32),
            pltpu.VMEM((channels // 128, TOKENS, 128), F32),
            pltpu.VMEM((TOKENS, channels), F32),
            pltpu.VMEM((TOKENS, channels), BF16),
            pltpu.VMEM((channels, 3 * channels), BF16),
            pltpu.VMEM((channels, channels), BF16),
            pltpu.VMEM((TOKENS, channels), BF16),
            pltpu.VMEM((TOKENS, 3 * channels), BF16),
            pltpu.VMEM((TOKENS, channels), BF16),
            pltpu.VMEM((TOKENS, channels), BF16),
            pltpu.VMEM((TOKENS, 3 * channels), BF16),
            pltpu.VMEM((channels // 128, TOKENS, 128), F32),
        ],
        24 << 20,
    )(where, shifts, region, tokens, cotangent, lat0, lat1, lon, corner, wqkv, wproj, gain, *others)


def on_device(sizes, tokens, cotangent, wqkv, wproj, gain, shifts, region):
    tokens = tokens.transpose(1, 2, 0, 3)
    cotangent = cotangent.transpose(1, 2, 0, 3)
    last = WIN_LON - 1
    channels = tokens.shape[-1]
    share = channels // 2
    lon_count = sizes["xl"] * sizes["zh"] * sizes["zl"] * sizes["c"]
    lat_count = sizes["y"] * sizes["xh"]

    struct = jax.ShapeDtypeStruct
    where = jnp.stack([lax.axis_index(a) for a in ("c", "xh", LAT, ("c", "zl"))]).astype(jnp.int32)
    most = WIN_LAT - 1
    part = share // 4
    wout = jnp.concatenate(
        [lax.dynamic_slice_in_dim(w, where[3] * part, part, 0) for w in (wqkv, wproj)], axis=1
    )
    early = 2
    wx = lax.ppermute(wout, ("xl", "xh"), BESIDE)
    lat = [
        jnp.stack([a[rows, :last] for a in (tokens, cotangent)])
        for rows in (slice(0, early), slice(early, most))
    ]
    lat[0] = lax.ppermute(lat[0], LAT, ring(lat_count, -1))
    lon = jnp.stack([a[:, last] for a in (tokens, cotangent)])
    lon = lax.ppermute(lon, LON, ring(lon_count, 1))
    foot = jnp.pad(gain.reshape(1, 1, share), ((0, 0), (0, LEVELS - 1), (0, channels - share)))
    corner = jnp.concatenate([tokens[:most, last], cotangent[:most, last], foot])
    corner = lax.ppermute(corner, LON + LAT, diagonal(lon_count, 1, lat_count, -1))
    wx, lat, lon, corner = lax.optimization_barrier((wx, lat, lon, corner))
    wz = lax.ppermute(wx, "zl", SWAP)
    lat[1] = lax.ppermute(lat[1], LAT, ring(lat_count, -1))
    wcx = lax.ppermute(wx, "c", SWAP)
    wz, wcx, lat = lax.optimization_barrier((wz, wcx, lat))
    wcz = lax.ppermute(wz, "c", SWAP)

    grid = struct(tokens.shape, BF16)
    block, grad, rlat, rlon, rcorner, keep, send = main_call(
        where, shifts, region, tokens, cotangent, *lat, lon, corner, wqkv, wproj, gain, wx, wz, wcx, wcz
    )

    pair = (keep.astype(F32) + lax.ppermute(send, "c", SWAP).astype(F32)).astype(BF16)
    plane = lax.all_to_all(pair, ("zl", "y", "xl", "xh"), 0, 0, tiled=True)
    piece = jnp.sum(plane.astype(F32), 0).astype(BF16)
    piece, rlat, rlon, rcorner = lax.optimization_barrier((piece, rlat, rlon, rcorner))
    rlat = lax.ppermute(rlat, LAT, ring(lat_count, 1))
    others = [lax.ppermute(piece, "zh", ring(4, by)) for by in (1, 2, 3)]
    rlon = lax.ppermute(rlon, LON, ring(lon_count, -1))
    rcorner = lax.ppermute(rcorner, LON + LAT, diagonal(lon_count, -1, lat_count, 1))
    others, rlat, rlon, rcorner = lax.optimization_barrier((others, rlat, rlon, rcorner))
    piece = (piece.astype(F32) + sum(p.astype(F32) for p in others)).astype(BF16)
    near = lax.all_to_all(
        jnp.broadcast_to(piece, (2 * COLUMNS,) + piece.shape), ("zl", "y", "xl"), 0, 0, tiled=True
    )
    far = lax.ppermute(near, "c", SWAP)

    out_block, out_grad = call(patch_kernel, [grid, grid], [SM] + [VM] * 7, moved=4 << 20)(
        shifts, tokens, cotangent, block, grad, rlat, rlon, rcorner
    )
    scaling = 1.0 / (TOKENS * lon_count * lat_count) ** 0.5
    half = share // 2
    of_rows = lambda z: (z, 0)
    of_pieces = pl.BlockSpec((COLUMNS, half, 128), lambda z: (z, 0, 0))
    of_gain = pl.BlockSpec((1, half), lambda z: (0, z))
    gqkv, gproj, ggain = pl.pallas_call(
        functools.partial(finish_kernel, scaling),
        grid=(2,),
        out_shape=[struct((share, 3 * channels), F32), struct((share, channels), F32), struct((1, share), F32)],
        in_specs=[SM, of_pieces, of_pieces, pl.BlockSpec((half, 3 * channels), of_rows), of_gain],
        out_specs=[
            pl.BlockSpec((half, 3 * channels), of_rows),
            pl.BlockSpec((half, channels), of_rows),
            of_gain,
        ],
        compiler_params=pltpu.CompilerParams(vmem_limit_bytes=12 << 20),
    )(where, near, far, wqkv, gain.reshape(1, share))
    return out_block.transpose(2, 0, 1, 3), out_grad.transpose(2, 0, 1, 3), gqkv, gproj, ggain.reshape(share)


def solution(mesh):
    lon, lat, fsdp = (mesh.shape[a] for a in ("lon", "lat", "fsdp"))
    sizes = {"xl": 2, "zh": lon // 8, "zl": 2, "c": 2, "y": lat, "xh": fsdp}
    fine = Mesh(mesh.devices.reshape(tuple(sizes.values())), tuple(sizes))
    grid = P(None, LAT, LON, None)
    rows = P("xh", None)
    return jax.shard_map(
        functools.partial(on_device, sizes),
        mesh=fine,
        in_specs=(grid, grid, rows, rows, P("xh"), P(), P()),
        out_specs=(grid, grid, rows, rows, P("xh")),
        check_vma=False,
    )
```

```python
import functools

import jax
import jax.numpy as jnp
from jax import lax
from jax.experimental import pallas as pl
from jax.experimental.pallas import tpu as pltpu
from jax.sharding import Mesh
from jax.sharding import PartitionSpec as P

HEADS = 16
HEAD = 32
GROUP = 8
SPAN = GROUP * HEAD
WIN_LAT = 6
WIN_LON = 12
LEVELS = 4
SLAB = WIN_LAT * WIN_LON
MEMBERS = 2 * SLAB
TOKENS = LEVELS * SLAB
COLUMNS = 8
norm_eps = 1e-05

F32 = jnp.float32
BF16 = jnp.bfloat16
NN = (((1,), (0,)), ((), ()))
NT = (((1,), (1,)), ((), ()))
TN = (((0,), (0,)), ((), ()))
VM = pl.BlockSpec(memory_space=pltpu.VMEM)
SM = pl.BlockSpec(memory_space=pltpu.SMEM)


def mul(a, b, how=NN):
    return lax.dot_general(a, b, how, preferred_element_type=F32)


def spread(block, lanes):
    zero = jnp.zeros_like(block)
    return jnp.concatenate([jnp.where(lanes == h, block, zero) for h in range(GROUP)], axis=0)


def fold(big, lanes):
    total = big[:MEMBERS]
    for h in range(1, GROUP):
        total = jnp.where(lanes == h, big[h * MEMBERS : (h + 1) * MEMBERS], total)
    return total


def label_of(member, rows, slot_is_last):
    second = (member >= SLAB).astype(jnp.int32)
    in_slab = member - SLAB * second
    label = jnp.zeros_like(member) + 2 * rows[0]
    for r in range(1, WIN_LAT):
        label = jnp.where(in_slab >= r * WIN_LON, 2 * rows[r], label)
    return label + second if slot_is_last else label


def main_kernel(
    where, shifts, region, tok, cot, lat0, lat1, lon, corner, wqkv, wproj, gain, wx, wz, wcx, wcz,
    block, grad, rlat, rlon, keep, send,
    xs, cs, xw, cw, wq, wp, hid, proj, dmix, mixed, dpro, ys,
):
    last = WIN_LON - 1
    channels = cw.shape[1]
    share = channels // 2
    half = share // 2
    core, f, here = where[0], where[1], where[2]

    own = pl.ds(pl.multiple_of(f * share, share), share)
    wq[own, :] = wqkv[...]
    wp[own, :] = wproj[...]
    quarter, at_x = wx.shape[0], where[3]
    for place, piece in ((at_x, wx), (at_x ^ 1, wz), (at_x ^ 2, wcx), (at_x ^ 3, wcz)):
        at = pl.ds(pl.multiple_of((1 - f) * share + place * quarter, quarter), quarter)
        wq[at, :] = piece[:, : 3 * channels]
        wp[at, :] = piece[:, 3 * channels :]
    near = gain[...].astype(F32).reshape(1, share)
    far = corner[2 * (WIN_LAT - 1)].astype(F32)[:1, :share]
    gains = jnp.concatenate(
        [jnp.where(f == 0, near, far), jnp.where(f == 0, far, near)], axis=1
    )

    def put(dst, r, c, got):
        at, got = (r * WIN_LON + c) * LEVELS, got.astype(F32)
        for q in range(channels // 128):
            dst[q, at : at + LEVELS, :] = got[:, q * 128 : (q + 1) * 128]

    most, by = WIN_LAT - 1, shifts[1]
    for r in range(WIN_LAT):
        if r < most:

            @pl.when(r < by)
            def _(r=r):
                for a, dst in enumerate((xs, cs)):
                    for c in range(last):
                        early = lat0.shape[1]
                        put(dst, r, c, lat0[a, r, c] if r < early else lat1[a, r - early, c])
                    put(dst, r, last, corner[a * most + r])

        @pl.when(r >= by)
        def _(r=r):
            for a, (src, dst) in enumerate(((tok, xs), (cot, cs))):
                for c in range(last):
                    put(dst, r, c, src[r, c])
                put(dst, r, last, lon[a, r])

    for slot in range(LEVELS):
        level = (slot + 1) % LEVELS
        at = slice(slot * SLAB, (slot + 1) * SLAB)
        for q in range(channels // 128):
            tile = slice(q * 128, (q + 1) * 128)
            xw[at, tile] = xs[q, pl.ds(level, SLAB, LEVELS), :]
            cw[at, tile] = cs[q, pl.ds(level, SLAB, LEVELS), :].astype(BF16)

    x = xw[...]
    mean = jnp.mean(x, -1, keepdims=True)
    cen = x - mean
    rstd = lax.rsqrt(jnp.mean(cen * cen, -1, keepdims=True) + norm_eps)
    hid[...] = (cen * rstd * gains).astype(BF16)
    proj[...] = mul(hid[...], wq[...]).astype(BF16)
    dmix[...] = mul(cw[...], wp[...], NT).astype(BF16)

    total = region.shape[0]
    regions = []
    for r in range(WIN_LAT):
        j = here + jnp.where(r < by, 1, 0)
        regions.append(region[lax.rem(j * WIN_LAT + r + total, total)])
    lane = lax.broadcasted_iota(jnp.int32, (1, GROUP * MEMBERS), 1)
    member = lane
    for h in range(1, GROUP):
        member = jnp.where(lane >= h * MEMBERS, lane - h * MEMBERS, member)
    down = lax.broadcasted_iota(jnp.int32, (MEMBERS, 1), 0)

    lanes = lax.broadcasted_iota(jnp.int32, (MEMBERS, SPAN), 1) // HEAD
    scale = 1.0 / HEAD**0.5
    to_exp2 = scale * 1.4426950408889634
    for w in range(2):
        rows = slice(w * MEMBERS, (w + 1) * MEMBERS)
        same = label_of(down, regions, w == 1) == label_of(member, regions, w == 1)
        for g in range(channels // SPAN):
            cols = slice(g * SPAN, (g + 1) * SPAN)
            kcols = slice(channels + g * SPAN, channels + (g + 1) * SPAN)
            vcols = slice(2 * channels + g * SPAN, 2 * channels + (g + 1) * SPAN)
            k, v = proj[rows, kcols], proj[rows, vcols]
            bq = spread(proj[rows, cols], lanes)
            s = jnp.where(same, mul(k, bq, NT), -1e30)
            e = jnp.exp2((s - jnp.max(s, 0, keepdims=True)) * to_exp2)
            p = e * (1.0 / jnp.sum(e, 0, keepdims=True))
            pb = p.astype(BF16)
            mixed[rows, cols] = fold(mul(pb, v, TN), lanes).astype(BF16)
            bm = spread(dmix[rows, cols], lanes)
            dp = mul(v, bm, NT)
            dpro[rows, vcols] = mul(pb, bm).astype(BF16)
            t = p * dp
            ds = ((t - p * jnp.sum(t, 0, keepdims=True)) * scale).astype(BF16)
            dpro[rows, kcols] = mul(ds, bq).astype(BF16)
            dpro[rows, cols] = fold(mul(ds, k, TN), lanes).astype(BF16)

    def give_back(values, a, base, out):
        for slot in range(LEVELS):
            for q in range(channels // 128):
                tile = values[slot * SLAB : (slot + 1) * SLAB, q * 128 : (q + 1) * 128]
                ys[q, pl.ds((slot + 1) % LEVELS, SLAB, LEVELS), :] = tile
        def made(r, c):
            at = (r * WIN_LON + c) * LEVELS
            tiles = [ys[q, at : at + LEVELS, :] for q in range(channels // 128)]
            return jnp.concatenate(tiles, axis=1).astype(BF16)

        for r in range(WIN_LAT):
            if r < most:

                @pl.when(r < by)
                def _(r=r):
                    for c in range(last):
                        rlat[a, r, c] = made(r, c)

            @pl.when(r >= by)
            def _(r=r):
                for c in range(last):
                    out[r, c] = (base[r, c].astype(F32) + made(r, c).astype(F32)).astype(BF16)

            rlon[a, r] = made(r, last)

    give_back(mul(mixed[...], wp[...]), 0, tok, block)

    wide, narrow = 3 * channels // 2, channels // 2
    for out, c in ((send, 1 - core), (keep, core)):
        dq = mul(hid[...], dpro[:, pl.ds(pl.multiple_of(c * wide, 128), wide)], TN)
        dw = mul(mixed[...], cw[:, pl.ds(pl.multiple_of(c * narrow, 128), narrow)], TN)
        for k in range(COLUMNS):
            part = dq[:, k * 128 : (k + 1) * 128] if k < 6 else dw[:, (k - 6) * 128 : (k - 5) * 128]
            for t in range(2):
                for z in range(2):
                    first = t * share + z * half
                    out[(z * COLUMNS + k) * 2 + t] = part[first : first + half].astype(BF16)

    dh = mul(dpro[...], wq[...], NT)
    xhat = (xw[...] - mean) * rstd
    dxhat = dh * gains
    low = jnp.mean(dxhat, -1, keepdims=True)
    tilt = jnp.mean(dxhat * xhat, -1, keepdims=True)
    give_back((dxhat - low - xhat * tilt) * rstd, 1, cot, grad)


def patch_kernel(shifts, tok, cot, block, grad, lat, lon, out_block, out_grad):
    last, most, by = WIN_LON - 1, WIN_LAT - 1, shifts[1]
    for a, (base, part, out) in enumerate(((tok, block, out_block), (cot, grad, out_grad))):
        for r in range(WIN_LAT):
            if r < most:

                @pl.when(r < by)
                def _(a=a, base=base, out=out, r=r):
                    got = lat[a, r].astype(F32)
                    out[r] = (base[r].astype(F32) + got).astype(BF16)

            @pl.when(r >= by)
            def _(a=a, base=base, part=part, out=out, r=r):
                out[r, :last] = part[r, :last]
                got = lon[a, r].astype(F32)
                out[r, last] = (base[r, last].astype(F32) + got).astype(BF16)


def finish_kernel(scaling, where, near, far, wqkv, gain, gqkv, gproj, ggain):
    core = where[0]
    rows, wide = gqkv.shape[0], gqkv.shape[1] // 2
    narrow = gproj.shape[1] // 2
    total = jnp.zeros((rows, 128), F32)
    for part, c in ((near, core), (far, 1 - core)):
        for k in range(COLUMNS):
            made = part[k].astype(F32) * scaling
            if k < 6:
                at = pl.ds(pl.multiple_of(c * wide + k * 128, 128), 128)
                gqkv[:, at] = made
                total = total + made * wqkv[:, at].astype(F32)
            else:
                gproj[:, pl.ds(pl.multiple_of(c * narrow + (k - 6) * 128, 128), 128)] = made
    over = jnp.sum(total.T, 0, keepdims=True)
    ggain[...] = over / gain[...].astype(F32)


def call(kernel, outs, ins, scratch=(), limit=12 << 20, moved=1 << 20):
    return pl.pallas_call(
        kernel,
        out_shape=outs,
        in_specs=ins,
        out_specs=[VM] * len(outs),
        scratch_shapes=list(scratch),
        compiler_params=pltpu.CompilerParams(vmem_limit_bytes=limit),
        cost_estimate=pl.CostEstimate(flops=0, bytes_accessed=moved, transcendentals=0),
    )


def ring(count, by):
    return [(i, (i + by) % count) for i in range(count)]


LON, LAT = ("xl", "zh", "zl", "c"), ("y", "xh")
SWAP = [(0, 1), (1, 0)]
BESIDE = [(0, 3), (3, 0), (1, 2), (2, 1)]


def diagonal(lon_count, by_lon, lat_count, by_lat):
    return [
        (o * lat_count + j, ((o + by_lon) % lon_count) * lat_count + (j + by_lat) % lat_count)
        for o in range(lon_count)
        for j in range(lat_count)
    ]


def main_call(where, shifts, region, tokens, cotangent, lat0, lat1, lon, corner, wqkv, wproj, gain, *others):
    struct = jax.ShapeDtypeStruct
    channels, share = tokens.shape[-1], wqkv.shape[0]
    grid = struct(tokens.shape, BF16)
    pieces = struct((4 * COLUMNS, share // 2, 128), BF16)
    rlat = struct((2, WIN_LAT - 1, WIN_LON, LEVELS, channels), BF16)
    return call(
        main_kernel,
        [grid, grid, rlat, struct(lon.shape, BF16), pieces, pieces],
        [SM, SM, SM] + [VM] * 13,
        [
            pltpu.VMEM((channels // 128, TOKENS, 128), F32),
            pltpu.VMEM((channels // 128, TOKENS, 128), F32),
            pltpu.VMEM((TOKENS, channels), F32),
            pltpu.VMEM((TOKENS, channels), BF16),
            pltpu.VMEM((channels, 3 * channels), BF16),
            pltpu.VMEM((channels, channels), BF16),
            pltpu.VMEM((TOKENS, channels), BF16),
            pltpu.VMEM((TOKENS, 3 * channels), BF16),
            pltpu.VMEM((TOKENS, channels), BF16),
            pltpu.VMEM((TOKENS, channels), BF16),
            pltpu.VMEM((TOKENS, 3 * channels), BF16),
            pltpu.VMEM((channels // 128, TOKENS, 128), F32),
        ],
        24 << 20,
    )(where, shifts, region, tokens, cotangent, lat0, lat1, lon, corner, wqkv, wproj, gain, *others)


def on_device(sizes, tokens, cotangent, wqkv, wproj, gain, shifts, region):
    tokens = tokens.transpose(1, 2, 0, 3)
    cotangent = cotangent.transpose(1, 2, 0, 3)
    last = WIN_LON - 1
    channels = tokens.shape[-1]
    share = channels // 2
    lon_count = sizes["xl"] * sizes["zh"] * sizes["zl"] * sizes["c"]
    lat_count = sizes["y"] * sizes["xh"]

    struct = jax.ShapeDtypeStruct
    where = jnp.stack([lax.axis_index(a) for a in ("c", "xh", LAT, ("c", "zl"))]).astype(jnp.int32)
    most = WIN_LAT - 1
    part = share // 4
    wout = jnp.concatenate(
        [lax.dynamic_slice_in_dim(w, where[3] * part, part, 0) for w in (wqkv, wproj)], axis=1
    )
    early = 2
    wx = lax.ppermute(wout, ("xl", "xh"), BESIDE)
    lat = [
        jnp.stack([a[rows, :last] for a in (tokens, cotangent)])
        for rows in (slice(0, early), slice(early, most))
    ]
    lat[0] = lax.ppermute(lat[0], LAT, ring(lat_count, -1))
    lon = jnp.stack([a[:, last] for a in (tokens, cotangent)])
    lon = lax.ppermute(lon, LON, ring(lon_count, 1))
    foot = jnp.pad(gain.reshape(1, 1, share), ((0, 0), (0, LEVELS - 1), (0, channels - share)))
    corner = jnp.concatenate([tokens[:most, last], cotangent[:most, last], foot])
    corner = lax.ppermute(corner, LON + LAT, diagonal(lon_count, 1, lat_count, -1))
    wx, lat, lon, corner = lax.optimization_barrier((wx, lat, lon, corner))
    wz = lax.ppermute(wx, "zl", SWAP)
    lat[1] = lax.ppermute(lat[1], LAT, ring(lat_count, -1))
    wcx = lax.ppermute(wx, "c", SWAP)
    wz, wcx, lat = lax.optimization_barrier((wz, wcx, lat))
    wcz = lax.ppermute(wz, "c", SWAP)

    grid = struct(tokens.shape, BF16)
    block, grad, rlat, rlon, keep, send = main_call(
        where, shifts, region, tokens, cotangent, *lat, lon, corner, wqkv, wproj, gain, wx, wz, wcx, wcz
    )

    arrived = lax.ppermute(send, "c", SWAP)
    rlon = lax.ppermute(rlon, LON, ring(lon_count, -1))
    arrived, rlon = lax.optimization_barrier((arrived, rlon))
    pair = (keep.astype(F32) + arrived.astype(F32)).astype(BF16)
    plane = lax.all_to_all(pair, ("zl", "y", "xl", "xh"), 0, 0, tiled=True)
    piece = jnp.sum(plane.astype(F32), 0).astype(BF16)
    piece, rlat, rlon = lax.optimization_barrier((piece, rlat, rlon))
    rlat = rlat.at[:, :, last].set(rlon[:, :most])
    rlat = lax.ppermute(rlat, LAT, ring(lat_count, 1))
    others = jnp.broadcast_to(piece, (sizes["zh"],) + piece.shape)
    others = lax.all_to_all(others, "zh", 0, 0, tiled=True)
    others, rlat = lax.optimization_barrier((others, rlat))
    piece = jnp.sum(others.astype(F32), 0).astype(BF16)
    near = lax.all_to_all(
        jnp.broadcast_to(piece, (2 * COLUMNS,) + piece.shape), ("zl", "y", "xl"), 0, 0, tiled=True
    )
    far = lax.ppermute(near, "c", SWAP)

    out_block, out_grad = call(patch_kernel, [grid, grid], [SM] + [VM] * 6, moved=4 << 20)(
        shifts, tokens, cotangent, block, grad, rlat, rlon
    )
    scaling = 1.0 / (TOKENS * lon_count * lat_count) ** 0.5
    half = share // 2
    of_rows = lambda z: (z, 0)
    of_pieces = pl.BlockSpec((COLUMNS, half, 128), lambda z: (z, 0, 0))
    of_gain = pl.BlockSpec((1, half), lambda z: (0, z))
    gqkv, gproj, ggain = pl.pallas_call(
        functools.partial(finish_kernel, scaling),
        grid=(2,),
        out_shape=[struct((share, 3 * channels), F32), struct((share, channels), F32), struct((1, share), F32)],
        in_specs=[SM, of_pieces, of_pieces, pl.BlockSpec((half, 3 * channels), of_rows), of_gain],
        out_specs=[
            pl.BlockSpec((half, 3 * channels), of_rows),
            pl.BlockSpec((half, channels), of_rows),
            of_gain,
        ],
        compiler_params=pltpu.CompilerParams(vmem_limit_bytes=12 << 20),
    )(where, near, far, wqkv, gain.reshape(1, share))
    return out_block.transpose(2, 0, 1, 3), out_grad.transpose(2, 0, 1, 3), gqkv, gproj, ggain.reshape(share)


def solution(mesh):
    lon, lat, fsdp = (mesh.shape[a] for a in ("lon", "lat", "fsdp"))
    sizes = {"xl": 2, "zh": lon // 8, "zl": 2, "c": 2, "y": lat, "xh": fsdp}
    fine = Mesh(mesh.devices.reshape(tuple(sizes.values())), tuple(sizes))
    grid = P(None, LAT, LON, None)
    rows = P("xh", None)
    return jax.shard_map(
        functools.partial(on_device, sizes),
        mesh=fine,
        in_specs=(grid, grid, rows, rows, P("xh"), P(), P()),
        out_specs=(grid, grid, rows, rows, P("xh")),
        check_vma=False,
    )
```

```python
import functools

import jax
import jax.numpy as jnp
from jax import lax
from jax.experimental import pallas as pl
from jax.experimental.pallas import tpu as pltpu
from jax.sharding import Mesh
from jax.sharding import PartitionSpec as P

HEADS = 16
HEAD = 32
GROUP = 8
SPAN = GROUP * HEAD
WIN_LAT = 6
WIN_LON = 12
LEVELS = 4
SLAB = WIN_LAT * WIN_LON
MEMBERS = 2 * SLAB
TOKENS = LEVELS * SLAB
COLUMNS = 8
norm_eps = 1e-05

F32 = jnp.float32
BF16 = jnp.bfloat16
NN = (((1,), (0,)), ((), ()))
NT = (((1,), (1,)), ((), ()))
TN = (((0,), (0,)), ((), ()))
VM = pl.BlockSpec(memory_space=pltpu.VMEM)
SM = pl.BlockSpec(memory_space=pltpu.SMEM)


def mul(a, b, how=NN):
    return lax.dot_general(a, b, how, preferred_element_type=F32)


def spread(block, lanes):
    zero = jnp.zeros_like(block)
    return jnp.concatenate([jnp.where(lanes == h, block, zero) for h in range(GROUP)], axis=0)


def fold(big, lanes):
    total = big[:MEMBERS]
    for h in range(1, GROUP):
        total = jnp.where(lanes == h, big[h * MEMBERS : (h + 1) * MEMBERS], total)
    return total


def label_of(member, rows, slot_is_last):
    second = (member >= SLAB).astype(jnp.int32)
    in_slab = member - SLAB * second
    label = jnp.zeros_like(member) + 2 * rows[0]
    for r in range(1, WIN_LAT):
        label = jnp.where(in_slab >= r * WIN_LON, 2 * rows[r], label)
    return label + second if slot_is_last else label


def main_kernel(
    where, shifts, region, tok, cot, lat0, lat1, lon, corner, wqkv, wproj, gain, wx, wz, wcx, wcz,
    block, grad, rlat, rlon, rcorner, keep, send,
    xs, cs, xw, cw, wq, wp, hid, proj, dmix, mixed, dpro, ys,
):
    last = WIN_LON - 1
    channels = cw.shape[1]
    share = channels // 2
    half = share // 2
    core, f, here = where[0], where[1], where[2]

    own = pl.ds(pl.multiple_of(f * share, share), share)
    wq[own, :] = wqkv[...]
    wp[own, :] = wproj[...]
    quarter, at_x = wx.shape[0], where[3]
    for place, piece in ((at_x, wx), (at_x ^ 1, wz), (at_x ^ 2, wcx), (at_x ^ 3, wcz)):
        at = pl.ds(pl.multiple_of((1 - f) * share + place * quarter, quarter), quarter)
        wq[at, :] = piece[:, : 3 * channels]
        wp[at, :] = piece[:, 3 * channels :]
    near = gain[...].astype(F32).reshape(1, share)
    far = corner[2 * (WIN_LAT - 1)].astype(F32)[:1, :share]
    gains = jnp.concatenate(
        [jnp.where(f == 0, near, far), jnp.where(f == 0, far, near)], axis=1
    )

    def put(dst, r, c, got):
        at, got = (r * WIN_LON + c) * LEVELS, got.astype(F32)
        for q in range(channels // 128):
            dst[q, at : at + LEVELS, :] = got[:, q * 128 : (q + 1) * 128]

    most, by = WIN_LAT - 1, shifts[1]
    for r in range(WIN_LAT):
        if r < most:

            @pl.when(r < by)
            def _(r=r):
                for a, dst in enumerate((xs, cs)):
                    for c in range(last):
                        early = lat0.shape[1]
                        put(dst, r, c, lat0[a, r, c] if r < early else lat1[a, r - early, c])
                    put(dst, r, last, corner[a * most + r])

        @pl.when(r >= by)
        def _(r=r):
            for a, (src, dst) in enumerate(((tok, xs), (cot, cs))):
                for c in range(last):
                    put(dst, r, c, src[r, c])
                put(dst, r, last, lon[a, r])

    for slot in range(LEVELS):
        level = (slot + 1) % LEVELS
        at = slice(slot * SLAB, (slot + 1) * SLAB)
        for q in range(channels // 128):
            tile = slice(q * 128, (q + 1) * 128)
            xw[at, tile] = xs[q, pl.ds(level, SLAB, LEVELS), :]
            cw[at, tile] = cs[q, pl.ds(level, SLAB, LEVELS), :].astype(BF16)

    x = xw[...]
    mean = jnp.mean(x, -1, keepdims=True)
    cen = x - mean
    rstd = lax.rsqrt(jnp.mean(cen * cen, -1, keepdims=True) + norm_eps)
    hid[...] = (cen * rstd * gains).astype(BF16)
    proj[...] = mul(hid[...], wq[...]).astype(BF16)
    dmix[...] = mul(cw[...], wp[...], NT).astype(BF16)

    total = region.shape[0]
    regions = []
    for r in range(WIN_LAT):
        j = here + jnp.where(r < by, 1, 0)
        regions.append(region[lax.rem(j * WIN_LAT + r + total, total)])
    lane = lax.broadcasted_iota(jnp.int32, (1, GROUP * MEMBERS), 1)
    member = lane
    for h in range(1, GROUP):
        member = jnp.where(lane >= h * MEMBERS, lane - h * MEMBERS, member)
    down = lax.broadcasted_iota(jnp.int32, (MEMBERS, 1), 0)

    lanes = lax.broadcasted_iota(jnp.int32, (MEMBERS, SPAN), 1) // HEAD
    scale = 1.0 / HEAD**0.5
    to_exp2 = scale * 1.4426950408889634
    for w in range(2):
        rows = slice(w * MEMBERS, (w + 1) * MEMBERS)
        same = label_of(down, regions, w == 1) == label_of(member, regions, w == 1)
        for g in range(channels // SPAN):
            cols = slice(g * SPAN, (g + 1) * SPAN)
            kcols = slice(channels + g * SPAN, channels + (g + 1) * SPAN)
            vcols = slice(2 * channels + g * SPAN, 2 * channels + (g + 1) * SPAN)
            k, v = proj[rows, kcols], proj[rows, vcols]
            bq = spread(proj[rows, cols], lanes)
            s = jnp.where(same, mul(k, bq, NT), -1e30)
            e = jnp.exp2((s - jnp.max(s, 0, keepdims=True)) * to_exp2)
            p = e * (1.0 / jnp.sum(e, 0, keepdims=True))
            pb = p.astype(BF16)
            mixed[rows, cols] = fold(mul(pb, v, TN), lanes).astype(BF16)
            bm = spread(dmix[rows, cols], lanes)
            dp = mul(v, bm, NT)
            dpro[rows, vcols] = mul(pb, bm).astype(BF16)
            t = p * dp
            ds = ((t - p * jnp.sum(t, 0, keepdims=True)) * scale).astype(BF16)
            dpro[rows, kcols] = mul(ds, bq).astype(BF16)
            dpro[rows, cols] = fold(mul(ds, k, TN), lanes).astype(BF16)

    def give_back(values, a, base, out):
        for slot in range(LEVELS):
            for q in range(channels // 128):
                tile = values[slot * SLAB : (slot + 1) * SLAB, q * 128 : (q + 1) * 128]
                ys[q, pl.ds((slot + 1) % LEVELS, SLAB, LEVELS), :] = tile
        def made(r, c):
            at = (r * WIN_LON + c) * LEVELS
            tiles = [ys[q, at : at + LEVELS, :] for q in range(channels // 128)]
            return jnp.concatenate(tiles, axis=1).astype(BF16)

        for r in range(WIN_LAT):
            if r < most:

                @pl.when(r < by)
                def _(r=r):
                    for c in range(last):
                        rlat[a, r, c] = made(r, c)
                    rcorner[a * most + r] = made(r, last)

            @pl.when(r >= by)
            def _(r=r):
                for c in range(last):
                    out[r, c] = (base[r, c].astype(F32) + made(r, c).astype(F32)).astype(BF16)
                rlon[a, r] = made(r, last)

    give_back(mul(mixed[...], wp[...]), 0, tok, block)

    wide, narrow = 3 * channels // 2, channels // 2
    for out, c in ((send, 1 - core), (keep, core)):
        dq = mul(hid[...], dpro[:, pl.ds(pl.multiple_of(c * wide, 128), wide)], TN)
        dw = mul(mixed[...], cw[:, pl.ds(pl.multiple_of(c * narrow, 128), narrow)], TN)
        for k in range(COLUMNS):
            part = dq[:, k * 128 : (k + 1) * 128] if k < 6 else dw[:, (k - 6) * 128 : (k - 5) * 128]
            for t in range(2):
                for z in range(2):
                    first = t * share + z * half
                    out[(z * COLUMNS + k) * 2 + t] = part[first : first + half].astype(BF16)

    dh = mul(dpro[...], wq[...], NT)
    xhat = (xw[...] - mean) * rstd
    dxhat = dh * gains
    low = jnp.mean(dxhat, -1, keepdims=True)
    tilt = jnp.mean(dxhat * xhat, -1, keepdims=True)
    give_back((dxhat - low - xhat * tilt) * rstd, 1, cot, grad)


def patch_kernel(shifts, tok, cot, block, grad, lat, lon, corner, out_block, out_grad):
    last, most, by = WIN_LON - 1, WIN_LAT - 1, shifts[1]
    for a, (base, part, out) in enumerate(((tok, block, out_block), (cot, grad, out_grad))):
        for r in range(WIN_LAT):
            if r < most:

                @pl.when(r < by)
                def _(a=a, base=base, out=out, r=r):
                    got = lat[a, r].astype(F32)
                    out[r, :last] = (base[r, :last].astype(F32) + got).astype(BF16)
                    got = corner[a * most + r].astype(F32)
                    out[r, last] = (base[r, last].astype(F32) + got).astype(BF16)

            @pl.when(r >= by)
            def _(a=a, base=base, part=part, out=out, r=r):
                out[r, :last] = part[r, :last]
                got = lon[a, r].astype(F32)
                out[r, last] = (base[r, last].astype(F32) + got).astype(BF16)


def finish_kernel(scaling, where, near, far, wqkv, gain, gqkv, gproj, ggain):
    core = where[0]
    rows, wide = gqkv.shape[0], gqkv.shape[1] // 2
    narrow = gproj.shape[1] // 2
    total = jnp.zeros((rows, 128), F32)
    for part, c in ((near, core), (far, 1 - core)):
        for k in range(COLUMNS):
            made = part[k].astype(F32) * scaling
            if k < 6:
                at = pl.ds(pl.multiple_of(c * wide + k * 128, 128), 128)
                gqkv[:, at] = made
                total = total + made * wqkv[:, at].astype(F32)
            else:
                gproj[:, pl.ds(pl.multiple_of(c * narrow + (k - 6) * 128, 128), 128)] = made
    over = jnp.sum(total.T, 0, keepdims=True)
    ggain[...] = over / gain[...].astype(F32)


def call(kernel, outs, ins, scratch=(), limit=12 << 20, moved=1 << 20):
    return pl.pallas_call(
        kernel,
        out_shape=outs,
        in_specs=ins,
        out_specs=[VM] * len(outs),
        scratch_shapes=list(scratch),
        compiler_params=pltpu.CompilerParams(vmem_limit_bytes=limit),
        cost_estimate=pl.CostEstimate(flops=0, bytes_accessed=moved, transcendentals=0),
    )


def ring(count, by):
    return [(i, (i + by) % count) for i in range(count)]


LON, LAT = ("xl", "zh", "zl", "c"), ("y", "xh")
SWAP = [(0, 1), (1, 0)]
BESIDE = [(0, 3), (3, 0), (1, 2), (2, 1)]


def diagonal(lon_count, by_lon, lat_count, by_lat):
    return [
        (o * lat_count + j, ((o + by_lon) % lon_count) * lat_count + (j + by_lat) % lat_count)
        for o in range(lon_count)
        for j in range(lat_count)
    ]


def main_call(where, shifts, region, tokens, cotangent, lat0, lat1, lon, corner, wqkv, wproj, gain, *others):
    struct = jax.ShapeDtypeStruct
    channels, share = tokens.shape[-1], wqkv.shape[0]
    grid = struct(tokens.shape, BF16)
    pieces = struct((4 * COLUMNS, share // 2, 128), BF16)
    rlat = struct((2, WIN_LAT - 1, WIN_LON - 1, LEVELS, channels), BF16)
    rcorner = struct((2 * (WIN_LAT - 1), LEVELS, channels), BF16)
    return call(
        main_kernel,
        [grid, grid, rlat, struct(lon.shape, BF16), rcorner, pieces, pieces],
        [SM, SM, SM] + [VM] * 13,
        [
            pltpu.VMEM((channels // 128, TOKENS, 128), F32),
            pltpu.VMEM((channels // 128, TOKENS, 128), F32),
            pltpu.VMEM((TOKENS, channels), F32),
            pltpu.VMEM((TOKENS, channels), BF16),
            pltpu.VMEM((channels, 3 * channels), BF16),
            pltpu.VMEM((channels, channels), BF16),
            pltpu.VMEM((TOKENS, channels), BF16),
            pltpu.VMEM((TOKENS, 3 * channels), BF16),
            pltpu.VMEM((TOKENS, channels), BF16),
            pltpu.VMEM((TOKENS, channels), BF16),
            pltpu.VMEM((TOKENS, 3 * channels), BF16),
            pltpu.VMEM((channels // 128, TOKENS, 128), F32),
        ],
        24 << 20,
    )(where, shifts, region, tokens, cotangent, lat0, lat1, lon, corner, wqkv, wproj, gain, *others)


def on_device(sizes, tokens, cotangent, wqkv, wproj, gain, shifts, region):
    tokens = tokens.transpose(1, 2, 0, 3)
    cotangent = cotangent.transpose(1, 2, 0, 3)
    last = WIN_LON - 1
    channels = tokens.shape[-1]
    share = channels // 2
    lon_count = sizes["xl"] * sizes["zh"] * sizes["zl"] * sizes["c"]
    lat_count = sizes["y"] * sizes["xh"]

    struct = jax.ShapeDtypeStruct
    where = jnp.stack([lax.axis_index(a) for a in ("c", "xh", LAT, ("c", "zl"))]).astype(jnp.int32)
    most = WIN_LAT - 1
    part = share // 4
    wout = jnp.concatenate(
        [lax.dynamic_slice_in_dim(w, where[3] * part, part, 0) for w in (wqkv, wproj)], axis=1
    )
    early = 2
    wx = lax.ppermute(wout, ("xl", "xh"), BESIDE)
    lat = [
        jnp.stack([a[rows] for a in (tokens, cotangent)])
        for rows in (slice(0, early), slice(early, most))
    ]
    lat[0] = lax.ppermute(lat[0], LAT, ring(lat_count, -1))
    lon = jnp.stack([a[:, last] for a in (tokens, cotangent)])
    lon = lax.ppermute(lon, LON, ring(lon_count, 1))
    foot = jnp.pad(gain.reshape(1, 1, share), ((0, 0), (0, LEVELS - 1), (0, channels - share)))
    corner = jnp.concatenate([tokens[:most, last], cotangent[:most, last], foot])
    corner = lax.ppermute(corner, LON + LAT, diagonal(lon_count, 1, lat_count, -1))
    wx, lat, lon, corner = lax.optimization_barrier((wx, lat, lon, corner))
    wz = lax.ppermute(wx, "zl", SWAP)
    lat[1] = lax.ppermute(lat[1], LAT, ring(lat_count, -1))
    wcx = lax.ppermute(wx, "c", SWAP)
    wz, wcx, lat = lax.optimization_barrier((wz, wcx, lat))
    wcz = lax.ppermute(wz, "c", SWAP)

    grid = struct(tokens.shape, BF16)
    block, grad, rlat, rlon, rcorner, keep, send = main_call(
        where, shifts, region, tokens, cotangent, *lat, lon, corner, wqkv, wproj, gain, wx, wz, wcx, wcz
    )

    pair = (keep.astype(F32) + lax.ppermute(send, "c", SWAP).astype(F32)).astype(BF16)
    plane = lax.all_to_all(pair, ("zl", "y", "xl", "xh"), 0, 0, tiled=True)
    piece = jnp.sum(plane.astype(F32), 0).astype(BF16)
    piece, rlat, rlon, rcorner = lax.optimization_barrier((piece, rlat, rlon, rcorner))
    rlat = lax.ppermute(rlat, LAT, ring(lat_count, 1))
    others = [lax.ppermute(piece, "zh", ring(4, by)) for by in (1, 2, 3)]
    rlon = lax.ppermute(rlon, LON, ring(lon_count, -1))
    rcorner = lax.ppermute(rcorner, LON + LAT, diagonal(lon_count, -1, lat_count, 1))
    others, rlat, rlon, rcorner = lax.optimization_barrier((others, rlat, rlon, rcorner))
    piece = (piece.astype(F32) + sum(p.astype(F32) for p in others)).astype(BF16)
    near = lax.all_to_all(
        jnp.broadcast_to(piece, (2 * COLUMNS,) + piece.shape), ("zl", "y", "xl"), 0, 0, tiled=True
    )
    far = lax.ppermute(near, "c", SWAP)

    out_block, out_grad = call(patch_kernel, [grid, grid], [SM] + [VM] * 7, moved=4 << 20)(
        shifts, tokens, cotangent, block, grad, rlat, rlon, rcorner
    )
    scaling = 1.0 / (TOKENS * lon_count * lat_count) ** 0.5
    half = share // 2
    of_rows = lambda z: (z, 0)
    of_pieces = pl.BlockSpec((COLUMNS, half, 128), lambda z: (z, 0, 0))
    of_gain = pl.BlockSpec((1, half), lambda z: (0, z))
    gqkv, gproj, ggain = pl.pallas_call(
        functools.partial(finish_kernel, scaling),
        grid=(2,),
        out_shape=[struct((share, 3 * channels), F32), struct((share, channels), F32), struct((1, share), F32)],
        in_specs=[SM, of_pieces, of_pieces, pl.BlockSpec((half, 3 * channels), of_rows), of_gain],
        out_specs=[
            pl.BlockSpec((half, 3 * channels), of_rows),
            pl.BlockSpec((half, channels), of_rows),
            of_gain,
        ],
        compiler_params=pltpu.CompilerParams(vmem_limit_bytes=12 << 20),
    )(where, near, far, wqkv, gain.reshape(1, share))
    return out_block.transpose(2, 0, 1, 3), out_grad.transpose(2, 0, 1, 3), gqkv, gproj, ggain.reshape(share)


def solution(mesh):
    lon, lat, fsdp = (mesh.shape[a] for a in ("lon", "lat", "fsdp"))
    sizes = {"xl": 2, "zh": lon // 8, "zl": 2, "c": 2, "y": lat, "xh": fsdp}
    fine = Mesh(mesh.devices.reshape(tuple(sizes.values())), tuple(sizes))
    grid = P(None, LAT, LON, None)
    rows = P("xh", None)
    return jax.shard_map(
        functools.partial(on_device, sizes),
        mesh=fine,
        in_specs=(grid, grid, rows, rows, P("xh"), P(), P()),
        out_specs=(grid, grid, rows, rows, P("xh")),
        check_vma=False,
    )
```
